256 devices in a mesh: dp: 16 (over y, x_lo, core), tensor: 16 (over z, x_hi).
Axes of the slice: x: 4 (x_hi: 2, x_lo: 2; x = x_hi * 2 + x_lo), y: 4, z: 8, core: 2. Of those that a mesh axis runs over, the one named last changes fastest.
Arguments:
- inputs: bfloat16 [2048, 4096], P('dp', 'tensor'), may hold values from -6 to 6
- gate_blocks: bfloat16 [16, 112, 128, 128], P('dp', 'tensor'), may hold values from -0.125 to 0.125
- up_blocks: bfloat16 [16, 112, 128, 128], P('dp', 'tensor'), may hold values from -0.125 to 0.125
- block_mask: int32 [32, 112], P(None, 'tensor'), may hold values from 0 to 1, as said below
- grad_hidden: bfloat16 [2048, 14336], P('dp', 'tensor'), may hold values from -6 to 6
Outputs:
- hidden: bfloat16 [2048, 14336], P('dp', 'tensor')
- grad_inputs: bfloat16 [2048, 4096], P('dp', 'tensor')
- grad_gate_blocks: bfloat16 [16, 112, 128, 128], P('dp', 'tensor')
- grad_up_blocks: bfloat16 [16, 112, 128, 128], P('dp', 'tensor')
The draws below stay inside these ranges and needn't reach their ends.
Inputs may be any that keep to these rules, and one draw needn't show every extreme that they name: Every column of block_mask holds exactly 16 ones; the number of ones in a row differs from row to row and may be anything from 0 to 112.
All inputs are finite; a program needn't handle non-finite values.
Results may differ from the reference program's by a relative error of at most 0.023.
Values may be sent and summed in bfloat16 or wider, within the bound.
A program may use at most 128 MiB of HBM per device.

```python
import jax
import jax.numpy as jnp
from jax import lax

D = 4096
FF = 14336
BLOCK = 128
TOK_DEV = 128
RB = 32
CB = 112
KEEP = 16
TOKENS = 2048
N_DP = 16


def draw_block_mask(key, part):
    key = jax.random.fold_in(key, 7)
    col_keys = jax.random.split(key, CB)
    orders = jax.vmap(lambda one_key: jax.random.permutation(one_key, RB))(col_keys)
    kept_rows = orders[:, :KEEP]
    row_ids = jnp.arange(RB, dtype=jnp.int32)
    marked = jnp.any(kept_rows[:, :, None] == row_ids[None, None, :], axis=1)
    return jnp.transpose(marked).astype(jnp.int32)


def block_scale(stream_key, extent, cuts, smallest, top_value):
    gain = 1.0
    for position, parts in cuts:
        steps = jax.random.uniform(jax.random.fold_in(jax.random.fold_in(stream_key, 6), position), (parts,), jnp.float32, smallest / len(cuts), top_value / len(cuts))
        gain = gain * jnp.repeat(jnp.exp(steps), extent[position] // parts).reshape((-1,) + (1,) * (len(extent) - 1 - position))
    return gain


def bell_draw(key, shape, spread, reach, pieces=(), kind=jnp.bfloat16):
    entries = jax.random.normal(key, shape, jnp.float32) * spread
    if len(pieces) > 0:
        entries = block_scale(key, shape, pieces, -0.22, 0.18) * entries
    return jnp.clip(entries, min=-reach, max=reach).astype(kind)


def setup_inputs(seed: int = 0) -> dict:
    splits = jax.random.split(jax.random.key(seed), 6)
    inputs = bell_draw(splits[0], (TOKENS, D), 1.0, 6.0, ((0, 16), (1, 16)))
    gate_blocks = bell_draw(splits[1], (KEEP, CB, BLOCK, BLOCK), (KEEP * BLOCK) ** -0.5, 0.125, ((0, 16), (1, 16)))
    up_blocks = bell_draw(splits[2], (KEEP, CB, BLOCK, BLOCK), (KEEP * BLOCK) ** -0.5, 0.125, ((0, 16), (1, 16)))
    block_mask = draw_block_mask(jax.random.fold_in(splits[5], 71), 0)
    grad_hidden = bell_draw(splits[4], (TOKENS, FF), 1.0, 6.0, ((0, 16), (1, 16)))
    return dict(inputs=inputs, gate_blocks=gate_blocks, up_blocks=up_blocks, block_mask=block_mask, grad_hidden=grad_hidden)


def tables(block_mask):
    row_rank = jnp.cumsum(block_mask, axis=0) - 1
    levels = jnp.arange(KEEP, dtype=jnp.int32)
    chosen = (block_mask[None] == 1) & (row_rank[None] == levels[:, None, None])
    row_ids = jnp.arange(block_mask.shape[0], dtype=jnp.int32)
    row_index = jnp.sum(jnp.where(chosen, row_ids[None, :, None], 0), axis=1).astype(jnp.int32)
    return row_index


def reference(inputs, gate_blocks, up_blocks, block_mask, grad_hidden):
    row_index = tables(block_mask)
    blocks = inputs.reshape(TOKENS, RB, BLOCK)

    def forward(totals, level):
        gate_acc, up_acc = totals
        taken = jnp.take(blocks, row_index[level], axis=1).astype(jnp.float32)
        gate_acc = gate_acc + jnp.einsum("tcj,cjh->tch", taken, gate_blocks[level].astype(jnp.float32))
        up_acc = up_acc + jnp.einsum("tcj,cjh->tch", taken, up_blocks[level].astype(jnp.float32))
        return (gate_acc, up_acc), None

    empty = jnp.zeros((TOKENS, CB, BLOCK), jnp.float32)
    (gate_pre, up_pre), _ = lax.scan(forward, (empty, empty), jnp.arange(KEEP))
    sig_gate = jax.nn.sigmoid(gate_pre)
    hidden = (gate_pre * sig_gate * up_pre).astype(jnp.bfloat16)
    upstream = grad_hidden.reshape(TOKENS, CB, BLOCK).astype(jnp.float32)
    d_gate = (upstream * up_pre * sig_gate * (1.0 + gate_pre * (1.0 - sig_gate))).astype(jnp.bfloat16).astype(jnp.float32)
    d_up = (upstream * gate_pre * sig_gate).astype(jnp.bfloat16).astype(jnp.float32)
    grad_scale = TOKENS ** -0.5

    def partial_sum(taken, delta):
        terms = jnp.einsum("stcj,stch->scjh", taken, delta.reshape(N_DP, TOK_DEV, CB, BLOCK)) * grad_scale
        rounded = lax.optimization_barrier(terms.astype(jnp.bfloat16)).astype(jnp.float32)
        return jnp.sum(rounded, axis=0).astype(jnp.bfloat16)

    def backward(grad_acc, level):
        contrib = jnp.einsum("tch,cjh->tcj", d_gate, gate_blocks[level].astype(jnp.float32))
        contrib = contrib + jnp.einsum("tch,cjh->tcj", d_up, up_blocks[level].astype(jnp.float32))
        grad_acc = grad_acc.at[:, row_index[level], :].add(contrib)
        taken = jnp.take(blocks, row_index[level], axis=1).astype(jnp.float32).reshape(N_DP, TOK_DEV, CB, BLOCK)
        return grad_acc, (partial_sum(taken, d_gate), partial_sum(taken, d_up))

    grad_acc, (grad_gate_blocks, grad_up_blocks) = lax.scan(backward, jnp.zeros((TOKENS, RB, BLOCK), jnp.float32), jnp.arange(KEEP))
    grad_inputs = grad_acc.reshape(TOKENS, D).astype(jnp.bfloat16)
    return hidden.reshape(TOKENS, FF), grad_inputs, grad_gate_blocks, grad_up_blocks
```

```python
import jax
import jax.numpy as jnp
from jax import lax
from jax.experimental import pallas as pl
from jax.experimental.pallas import tpu as pltpu
from jax.sharding import PartitionSpec as P

MESH = pl.DeviceIdType.MESH
F32, BF16 = jnp.float32, jnp.bfloat16
B = 128
NC = 7
KEEP = 16
RB = 32
SCALE = 2048.0**-0.5


def kernel(
    x_ref, g_ref, u_ref, mask_ref, gh_ref,
    hid_ref, dx_ref, gg_ref, gu_ref,
    wbuf, xbuf, xt, dt, part_out, part_in, part, leave, land, up_s, up_r, dn_s, dn_r, last_s, last_r,
    rank, rows, following,
    ag_s, ag_r, in_s, in_r, rs_s, rs_r, dx_ss, dx_rs,
):
    dp, tn = lax.axis_index("dp"), lax.axis_index("tensor")
    y, x, k = dp // 4, (dp // 2) % 2, dp % 2
    z, h = tn // 2, tn % 2
    yp, ym, y2 = (y + 1) % 4, (y + 3) % 4, (y + 2) % 4
    zp, zm = (z + 1) % 8, (z + 7) % 8
    xo, ko, ho = 1 - x, 1 - k, 1 - h

    def slot(yy, xx, kk):
        return yy * 4 + xx * 2 + kk

    to_sib = (slot(y, x, ko), tn)
    to_x = (slot(y, xo, k), tn)
    to_yp = (slot(yp, x, k), tn)
    to_ym = (slot(ym, x, k), tn)
    to_zp = (dp, zp * 2 + h)
    to_zm = (dp, zm * 2 + h)
    to_h = (dp, z * 2 + ho)
    neighbours = (to_sib, to_x, to_yp, to_ym, to_zp, to_zm, to_h)

    barrier = pltpu.get_barrier_semaphore()
    for there in neighbours:
        pl.semaphore_signal(barrier, inc=1, device_id=there, device_id_type=MESH)

    for c in range(NC):
        wbuf[dp, c, 0] = g_ref[0, c]
        wbuf[dp, c, 1] = u_ref[0, c]
        wbuf[KEEP, c] = jnp.zeros((2, B, B), BF16)
    for b in range(2):
        xbuf[tn * 2 + b] = x_ref[:, b * B : (b + 1) * B]
    pl.semaphore_wait(barrier, len(neighbours))

    ring = ((y, x), (y, xo), (ym, x), (yp, x), (ym, xo), (yp, xo), (y2, x), (y2, xo))
    OWN, N, PP, MM, NP, NM, P2, M2 = range(8)

    def ag(kind, which, c, there, core):
        s = slot(*ring[which], core)
        return pltpu.make_async_remote_copy(
            src_ref=wbuf.at[s, c], dst_ref=wbuf.at[s, c],
            send_sem=ag_s.at[kind, c], recv_sem=ag_r.at[kind, c],
            device_id=there, device_id_type=MESH,
        )

    def ag_send(kind, which, c, there):
        ag(kind, which, c, there, k).start()

    def ag_got(kind, c):
        ag(kind, kind, c, to_x, k).wait_recv()

    def ag_share(which, c):
        ag(8 + which, which, c, to_sib, k).start()

    def ag_own(c):
        ag_send(N, OWN, c, to_x)
        ag_send(PP, OWN, c, to_yp)
        ag_send(MM, OWN, c, to_ym)
        ag_share(OWN, c)

    def ag_second(c):
        ag_got(N, c)
        ag_send(NP, N, c, to_yp)
        ag_send(NM, N, c, to_ym)
        ag_share(N, c)

    def ag_third(c):
        ag_got(PP, c)
        ag_send(P2, PP, c, to_yp)
        ag_share(PP, c)
        ag_got(MM, c)
        ag_share(MM, c)
        ag_got(NM, c)
        ag_send(M2, NM, c, to_ym)
        ag_share(NM, c)
        ag_got(NP, c)
        ag_share(NP, c)

    def ag_fourth(c):
        ag_got(P2, c)
        ag_share(P2, c)
        ag_got(M2, c)
        ag_share(M2, c)

    def ag_end(c):
        for which in range(8):
            ag(8 + which, which, c, to_sib, ko).wait_recv()

    def inp(sem, zz, hh, there):
        at = pl.ds(((zz + 8) % 8) * 4 + hh * 2, 2)
        return pltpu.make_async_remote_copy(
            src_ref=xbuf.at[at], dst_ref=xbuf.at[at],
            send_sem=in_s.at[sem], recv_sem=in_r.at[sem],
            device_id=there, device_id_type=MESH,
        )

    own_up, oth_dn, own_dn, oth_up = 0, 4, 8, 11

    inp(0, z, h, to_h).start()
    inp(own_up + 1, z, h, to_zp).start()
    inp(own_dn + 1, z, h, to_zm).start()
    for c in range(NC):
        ag_own(c)

    def column_tables(c, _):
        def count(r, seen):
            here = mask_ref[r, c]
            rank[r, c] = jnp.where(here == 1, jnp.minimum(seen, KEEP - 1), KEEP)
            return seen + here

        lax.fori_loop(0, RB, count, jnp.int32(0))

        def back(q, after):
            r = RB - 1 - q
            after = jnp.where(mask_ref[r, c] == 1, r, after)
            following[r] = after
            return after

        lax.fori_loop(0, RB, back, jnp.int32(RB - 1))

        def pick(kk, r):
            r = following[jnp.minimum(r, RB - 1)]
            rows[kk, c] = r
            return r + 1

        lax.fori_loop(0, KEEP, pick, jnp.int32(0))
        return 0

    lax.fori_loop(0, NC, column_tables, 0)

    inp(0, z, ho, to_h).wait_recv()
    inp(oth_up + 1, z, ho, to_zp).start()
    inp(oth_dn + 1, z, ho, to_zm).start()
    for j in (1, 2, 3, 4):
        inp(own_up + j, z - j, h, to_zp).wait_recv()
        if j < 4:
            inp(own_up + j + 1, z - j, h, to_zp).start()
        if j < 4:
            inp(own_dn + j, z + j, h, to_zm).wait_recv()
            if j < 3:
                inp(own_dn + j + 1, z + j, h, to_zm).start()
            inp(oth_up + j, z - j, ho, to_zp).wait_recv()
            if j < 3:
                inp(oth_up + j + 1, z - j, ho, to_zp).start()
        inp(oth_dn + j, z + j, ho, to_zm).wait_recv()
        if j < 4:
            inp(oth_dn + j + 1, z + j, ho, to_zm).start()
        for c in ((), (0, 1), (2, 3), (4, 5, 6), ())[j]:
            ag_second(c)
        for c in ((), (), (0,), (1,), ())[j]:
            ag_third(c)

    def turn(r, _):
        xt[r] = xbuf[r].T
        return 0

    lax.fori_loop(0, RB, turn, 0)
    ag_fourth(0)

    A_UP, A_DN, C_UP, C_DN, E_UP, F_DN, G_X = range(7)

    goal = ((y2, x), (y2, xo), (yp, xo), (ym, x), (yp, x), (ym, xo), (y, xo), (y, x))
    MINE = 7

    def rs(kind, c, there):
        return pltpu.make_async_remote_copy(
            src_ref=leave.at[kind, c], dst_ref=land.at[kind, c],
            send_sem=rs_s.at[kind, c], recv_sem=rs_r.at[kind, c],
            device_id=there, device_id_type=MESH,
        )

    def rs_pair(c):
        return pltpu.make_async_remote_copy(
            src_ref=part_out.at[c], dst_ref=part_in.at[c],
            send_sem=rs_s.at[7, c], recv_sem=rs_r.at[7, c],
            device_id=to_sib, device_id_type=MESH,
        )

    def rs_got(kind, c):
        rs(kind, c, to_x).wait_recv()

    def total(c, goes, kinds):
        value = part[c, goes].astype(F32) + part_in[c, goes].astype(F32)
        for kind in kinds:
            value = value + land[kind, c].astype(F32)
        return value

    def rs_send(kind, c, there, kinds=()):
        leave[kind, c] = total(c, kind, kinds).astype(BF16)
        rs(kind, c, there).start()

    def rs_first(c):
        rs_pair(c).wait_recv()
        rs_send(A_UP, c, to_yp)
        rs_send(A_DN, c, to_ym)
        rs_send(C_UP, c, to_yp)
        rs_send(C_DN, c, to_ym)

    def rs_second(c):
        rs_got(A_UP, c)
        rs_send(E_UP, c, to_yp, (A_UP,))
        rs_got(A_DN, c)
        rs_send(F_DN, c, to_ym, (A_DN,))

    def rs_third(c):
        rs_got(C_UP, c)
        rs_got(F_DN, c)
        rs_send(G_X, c, to_x, (C_UP, F_DN))

    def rs_last(c):
        for kind in (C_DN, E_UP, G_X):
            rs_got(kind, c)
        value = total(c, MINE, (C_DN, E_UP, G_X)).astype(BF16)
        gg_ref[0, c] = value[0]
        gu_ref[0, c] = value[1]

    def weight(s, c):
        return jnp.concatenate([wbuf[s, c, 0], wbuf[s, c, 1]], axis=1)

    def compute(c):
        acc = jnp.zeros((B, 2 * B), F32)
        for s in range(0, KEEP, 2):
            lhs = jnp.concatenate([xbuf[rows[s, c]], xbuf[rows[s + 1, c]]], axis=1)
            rhs = jnp.concatenate([weight(s, c), weight(s + 1, c)], axis=0)
            acc = acc + jnp.dot(lhs, rhs, preferred_element_type=F32)
        gate, up = acc[:, :B], acc[:, B:]
        sig = jax.nn.sigmoid(gate)
        silu = gate * sig
        lanes = pl.ds(pl.multiple_of(c * B, B), B)
        hid_ref[:, lanes] = (silu * up).astype(BF16)
        grad = gh_ref[:, lanes].astype(F32)
        d_gate = (grad * up * sig * (1.0 + gate * (1.0 - sig))).astype(BF16)
        d_up = (grad * silu).astype(BF16)
        dt[c, :B] = d_gate.T
        dt[c, B:] = d_up.T
        delta = jnp.concatenate([d_gate, d_up], axis=1)
        for core, target in ((ko, part_out), (k, part)):
            for i in range(0, 8, 2):
                blocks = [xt[rows[slot(*goal[i + half], core), c]] for half in range(2)]
                lhs = jnp.concatenate(blocks, axis=0)
                out = (jnp.dot(lhs, delta, preferred_element_type=F32) * SCALE).astype(BF16)
                for half in range(2):
                    target[c, i + half, 0] = out[half * B : (half + 1) * B, :B]
                    target[c, i + half, 1] = out[half * B : (half + 1) * B, B:]
            if target is part_out:
                rs_pair(c).start()

    def column(c, _):
        @pl.when(c + 2 < NC)
        def _():
            ag_third(c + 2)

        @pl.when(c + 1 < NC)
        def _():
            ag_fourth(c + 1)

        ag_end(c)
        compute(c)

        @pl.when(c >= 1)
        def _():
            rs_first(c - 1)

        @pl.when(c >= 2)
        def _():
            rs_second(c - 2)

        @pl.when(c >= 3)
        def _():
            rs_third(c - 3)

        @pl.when(c >= 4)
        def _():
            rs_last(c - 4)

        return 0

    lax.fori_loop(0, NC, column, 0)

    def unit(zz):
        def one(c, acc):
            lhs = jnp.concatenate([weight(rank[zz * 4 + b, c], c) for b in range(4)], axis=0)
            return acc + jnp.dot(lhs, dt[c], preferred_element_type=F32)

        return lax.fori_loop(0, NC, one, jnp.zeros((4 * B, B), F32)).reshape(4, B, B)

    def ring_copy(src, dst, sem, there):
        return pltpu.make_async_remote_copy(
            src_ref=src, dst_ref=dst, send_sem=dx_ss.at[sem], recv_sem=dx_rs.at[sem],
            device_id=there, device_id_type=MESH,
        )

    def go_up(n):
        cut = pl.ds(0, 2 if n == 0 else 4)
        return ring_copy(up_s.at[n, cut], up_r.at[n, cut], n, to_zp)

    def go_down(n):
        cut = pl.ds(2, 2) if n == 0 else pl.ds(0, 4)
        return ring_copy(dn_s.at[n, cut], dn_r.at[n, cut], 4 + n, to_zm)

    far = unit((z + 4) % 8).astype(BF16)
    up_s[0, :2] = far[:2]
    go_up(0).start()
    dn_s[0, 2:] = far[2:]
    go_down(0).start()

    def step(n):
        mine = unit((z + 4 - n) % 8)
        go_up(n - 1).wait_recv()
        if n == 1:
            up_s[n, :2] = (mine[:2] + up_r[0, :2].astype(F32)).astype(BF16)
            up_s[n, 2:] = mine[2:].astype(BF16)
        else:
            up_s[n] = (mine + up_r[n - 1].astype(F32)).astype(BF16)
        go_up(n).start()
        mine = unit((z + 4 + n) % 8)
        go_down(n - 1).wait_recv()
        if n == 1:
            dn_s[n, :2] = mine[:2].astype(BF16)
            dn_s[n, 2:] = (mine[2:] + dn_r[0, 2:].astype(F32)).astype(BF16)
        else:
            dn_s[n] = (mine + dn_r[n - 1].astype(F32)).astype(BF16)
        go_down(n).start()

    rs_first(NC - 1)
    rs_second(NC - 2)
    rs_third(NC - 3)
    rs_last(NC - 4)
    step(1)
    rs_second(NC - 1)
    rs_third(NC - 2)
    rs_last(NC - 3)
    step(2)
    rs_third(NC - 1)
    rs_last(NC - 2)
    step(3)
    mine = unit(z)
    go_up(3).wait_recv()
    go_down(3).wait_recv()
    last_s[...] = (mine + up_r[3].astype(F32) + dn_r[3].astype(F32)).astype(BF16)
    across = ring_copy(last_s.at[pl.ds(ho * 2, 2)], last_r, 8, to_h)
    across.start()
    rs_last(NC - 1)
    across.wait_recv()
    for b in range(2):
        value = last_s[h * 2 + b].astype(F32) + last_r[b].astype(F32)
        dx_ref[:, b * B : (b + 1) * B] = value.T.astype(BF16)

    def sent(c, _):
        for kind in range(1, 16):
            ag(kind, 0, c, to_x, k).wait_send()
        for kind in range(7):
            rs(kind, c, to_x).wait_send()
        rs_pair(c).wait_send()
        return 0

    lax.fori_loop(0, NC, sent, 0)
    for sem in range(15):
        inp(sem, z, h, to_h).wait_send()
    for n in range(4):
        go_up(n).wait_send()
        go_down(n).wait_send()
    across.wait_send()


def per_device(inputs, gate_blocks, up_blocks, block_mask, grad_hidden):
    vmem = pl.BlockSpec(memory_space=pltpu.VMEM)
    dma = pltpu.SemaphoreType.DMA
    unit = (4, B, B)
    return pl.pallas_call(
        kernel,
        out_shape=(
            jax.ShapeDtypeStruct(grad_hidden.shape, BF16),
            jax.ShapeDtypeStruct(inputs.shape, BF16),
            jax.ShapeDtypeStruct(gate_blocks.shape, BF16),
            jax.ShapeDtypeStruct(up_blocks.shape, BF16),
        ),
        in_specs=[vmem, vmem, vmem, pl.BlockSpec(memory_space=pltpu.SMEM), vmem],
        out_specs=(vmem, vmem, vmem, vmem),
        scratch_shapes=[
            pltpu.VMEM((KEEP + 1, NC, 2, B, B), BF16),
            pltpu.VMEM((RB, B, B), BF16),
            pltpu.VMEM((RB, B, B), BF16),
            pltpu.VMEM((NC, 2 * B, B), BF16),
            pltpu.VMEM((NC, 8, 2, B, B), BF16),
            pltpu.VMEM((NC, 8, 2, B, B), BF16),
            pltpu.VMEM((NC, 8, 2, B, B), BF16),
            pltpu.VMEM((7, NC, 2, B, B), BF16),
            pltpu.VMEM((7, NC, 2, B, B), BF16),
            pltpu.VMEM((4,) + unit, BF16),
            pltpu.VMEM((4,) + unit, BF16),
            pltpu.VMEM((4,) + unit, BF16),
            pltpu.VMEM((4,) + unit, BF16),
            pltpu.VMEM(unit, BF16),
            pltpu.VMEM((2, B, B), BF16),
            pltpu.SMEM((RB, NC), jnp.int32),
            pltpu.SMEM((KEEP, NC), jnp.int32),
            pltpu.SMEM((RB,), jnp.int32),
            dma((16, NC)),
            dma((16, NC)),
            dma((15,)),
            dma((15,)),
            dma((8, NC)),
            dma((8, NC)),
            dma((9,)),
            dma((9,)),
        ],
        compiler_params=pltpu.CompilerParams(
            collective_id=0, has_side_effects=True, vmem_limit_bytes=56 * 2**20
        ),
        cost_estimate=pl.CostEstimate(
            flops=4 * 10**9, bytes_accessed=3 * 2**20, transcendentals=128 * 896
        ),
    )(inputs, gate_blocks, up_blocks, block_mask, grad_hidden)


def solution(mesh):
    return jax.shard_map(
        per_device,
        mesh=mesh,
        in_specs=(
            P("dp", "tensor"),
            P("dp", "tensor", None, None),
            P("dp", "tensor", None, None),
            P(None, "tensor"),
            P("dp", "tensor"),
        ),
        out_specs=(
            P("dp", "tensor"),
            P("dp", "tensor"),
            P("dp", "tensor", None, None),
            P("dp", "tensor", None, None),
        ),
        check_vma=False,
    )
```

```python
import jax
import jax.numpy as jnp
from jax import lax
from jax.experimental import pallas as pl
from jax.experimental.pallas import tpu as pltpu
from jax.sharding import PartitionSpec as P

MESH = pl.DeviceIdType.MESH
F32, BF16 = jnp.float32, jnp.bfloat16
B = 128
NC = 7
KEEP = 16
RB = 32
SCALE = 2048.0**-0.5


def kernel(
    x_ref, g_ref, u_ref, mask_ref, gh_ref,
    hid_ref, dx_ref, gg_ref, gu_ref,
    wbuf, xbuf, xt, dt, part_out, part_in, part, leave, land, up_s, up_r, dn_s, dn_r, last_s, last_r,
    rank, rows, following,
    ag_s, ag_r, in_s, in_r, rs_s, rs_r, dx_ss, dx_rs,
):
    dp, tn = lax.axis_index("dp"), lax.axis_index("tensor")
    y, x, k = dp // 4, (dp // 2) % 2, dp % 2
    z, h = tn // 2, tn % 2
    yp, ym, y2 = (y + 1) % 4, (y + 3) % 4, (y + 2) % 4
    zp, zm = (z + 1) % 8, (z + 7) % 8
    xo, ko, ho = 1 - x, 1 - k, 1 - h

    def slot(yy, xx, kk):
        return yy * 4 + xx * 2 + kk

    to_sib = (slot(y, x, ko), tn)
    to_x = (slot(y, xo, k), tn)
    to_yp = (slot(yp, x, k), tn)
    to_ym = (slot(ym, x, k), tn)
    to_zp = (dp, zp * 2 + h)
    to_zm = (dp, zm * 2 + h)
    to_h = (dp, z * 2 + ho)
    neighbours = (to_sib, to_x, to_yp, to_ym, to_zp, to_zm, to_h)

    barrier = pltpu.get_barrier_semaphore()
    for there in neighbours:
        pl.semaphore_signal(barrier, inc=1, device_id=there, device_id_type=MESH)

    for c in range(NC):
        wbuf[dp, c, 0] = g_ref[0, c]
        wbuf[dp, c, 1] = u_ref[0, c]
        wbuf[KEEP, c] = jnp.zeros((2, B, B), BF16)
    for b in range(2):
        xbuf[tn * 2 + b] = x_ref[:, b * B : (b + 1) * B]
    pl.semaphore_wait(barrier, len(neighbours))

    ring = ((y, x), (y, xo), (ym, x), (yp, x), (ym, xo), (yp, xo), (y2, x), (y2, xo))
    OWN, N, PP, MM, NP, NM, P2, M2 = range(8)

    def ag(kind, which, c, there, core):
        s = slot(*ring[which], core)
        return pltpu.make_async_remote_copy(
            src_ref=wbuf.at[s, c], dst_ref=wbuf.at[s, c],
            send_sem=ag_s.at[kind, c], recv_sem=ag_r.at[kind, c],
            device_id=there, device_id_type=MESH,
        )

    def ag_send(kind, which, c, there):
        ag(kind, which, c, there, k).start()

    def ag_got(kind, c):
        ag(kind, kind, c, to_x, k).wait_recv()

    def ag_share(which, c):
        ag(8 + which, which, c, to_sib, k).start()

    def ag_own(c):
        ag_send(N, OWN, c, to_x)
        ag_send(PP, OWN, c, to_yp)
        ag_send(MM, OWN, c, to_ym)
        ag_share(OWN, c)

    def ag_second(c):
        ag_got(N, c)
        ag_send(NP, N, c, to_yp)
        ag_send(NM, N, c, to_ym)
        ag_share(N, c)

    def ag_third(c):
        ag_got(PP, c)
        ag_send(P2, PP, c, to_yp)
        ag_share(PP, c)
        ag_got(MM, c)
        ag_share(MM, c)
        ag_got(NM, c)
        ag_send(M2, NM, c, to_ym)
        ag_share(NM, c)
        ag_got(NP, c)
        ag_share(NP, c)

    def ag_fourth(c):
        ag_got(P2, c)
        ag_share(P2, c)
        ag_got(M2, c)
        ag_share(M2, c)

    HALF = 0

    def ag_half(kind, which, c, half, there):
        s = slot(*ring[which], k)
        return pltpu.make_async_remote_copy(
            src_ref=wbuf.at[s, c, half], dst_ref=wbuf.at[s, c, half],
            send_sem=ag_s.at[kind, c], recv_sem=ag_r.at[kind, c],
            device_id=there, device_id_type=MESH,
        )

    def ag_second_odd(c):
        ag_got(PP, c)
        ag_half(P2, PP, c, 0, to_yp).start()
        ag_send(NP, PP, c, to_x)
        ag_share(PP, c)
        ag_got(MM, c)
        ag_half(HALF, MM, c, 1, to_ym).start()
        ag_send(NM, MM, c, to_x)
        ag_share(MM, c)
        ag_got(N, c)
        ag_share(N, c)

    def ag_third_odd(c):
        ag_half(P2, P2, c, 0, to_yp).wait_recv()
        ag_half(HALF, P2, c, 1, to_ym).wait_recv()
        ag_send(M2, P2, c, to_x)
        ag_share(P2, c)
        ag_got(NP, c)
        ag_share(NP, c)
        ag_got(NM, c)
        ag_share(NM, c)

    def ag_fourth_odd(c):
        ag_got(M2, c)
        ag_share(M2, c)

    def either(c, even, odd):
        if isinstance(c, int):
            (odd if c % 2 else even)(c)
        else:
            pl.when(c % 2 == 0)(lambda: even(c))
            pl.when(c % 2 == 1)(lambda: odd(c))

    def ag_end(c):
        for which in range(8):
            ag(8 + which, which, c, to_sib, ko).wait_recv()

    def inp(sem, zz, hh, there):
        at = pl.ds(((zz + 8) % 8) * 4 + hh * 2, 2)
        return pltpu.make_async_remote_copy(
            src_ref=xbuf.at[at], dst_ref=xbuf.at[at],
            send_sem=in_s.at[sem], recv_sem=in_r.at[sem],
            device_id=there, device_id_type=MESH,
        )

    own_up, oth_dn, own_dn, oth_up = 0, 4, 8, 11

    inp(0, z, h, to_h).start()
    inp(own_up + 1, z, h, to_zp).start()
    inp(own_dn + 1, z, h, to_zm).start()
    for c in range(NC):
        ag_own(c)

    inp(0, z, ho, to_h).wait_recv()
    inp(oth_up + 1, z, ho, to_zp).start()
    inp(oth_dn + 1, z, ho, to_zm).start()

    def column_tables(c, _):
        def count(r, seen):
            here = mask_ref[r, c]
            rank[r, c] = jnp.where(here == 1, jnp.minimum(seen, KEEP - 1), KEEP)
            return seen + here

        lax.fori_loop(0, RB, count, jnp.int32(0))

        def back(q, after):
            r = RB - 1 - q
            after = jnp.where(mask_ref[r, c] == 1, r, after)
            following[r] = after
            return after

        lax.fori_loop(0, RB, back, jnp.int32(RB - 1))

        def pick(kk, r):
            r = following[jnp.minimum(r, RB - 1)]
            rows[kk, c] = r
            return r + 1

        lax.fori_loop(0, KEEP, pick, jnp.int32(0))
        return 0

    lax.fori_loop(0, NC, column_tables, 0)

    for j in (1, 2, 3, 4):
        inp(own_up + j, z - j, h, to_zp).wait_recv()
        if j < 4:
            inp(own_up + j + 1, z - j, h, to_zp).start()
        if j < 4:
            inp(own_dn + j, z + j, h, to_zm).wait_recv()
            if j < 3:
                inp(own_dn + j + 1, z + j, h, to_zm).start()
            inp(oth_up + j, z - j, ho, to_zp).wait_recv()
            if j < 3:
                inp(oth_up + j + 1, z - j, ho, to_zp).start()
        inp(oth_dn + j, z + j, ho, to_zm).wait_recv()
        if j < 4:
            inp(oth_dn + j + 1, z + j, ho, to_zm).start()
        for c in ((), (0, 1, 2), (3, 4, 5, 6), (), ())[j]:
            either(c, ag_second, ag_second_odd)
        for c in ((), (), (0,), (1, 2, 3), (4, 5))[j]:
            either(c, ag_third, ag_third_odd)
        for c in ((), (), (), (0,), (1,))[j]:
            either(c, ag_fourth, ag_fourth_odd)

    def turn(r, _):
        xt[r] = xbuf[r].T
        return 0

    lax.fori_loop(0, RB, turn, 0)
    ag_third(6)
    ag_fourth(2)

    A_UP, A_DN, C_UP, C_DN, E_UP, F_DN, G_X = range(7)

    goal = ((y2, x), (y2, xo), (yp, xo), (ym, x), (yp, x), (ym, xo), (y, xo), (y, x))
    MINE = 7

    def rs(kind, c, there):
        return pltpu.make_async_remote_copy(
            src_ref=leave.at[kind, c], dst_ref=land.at[kind, c],
            send_sem=rs_s.at[kind, c], recv_sem=rs_r.at[kind, c],
            device_id=there, device_id_type=MESH,
        )

    def rs_pair(c):
        return pltpu.make_async_remote_copy(
            src_ref=part_out.at[c], dst_ref=part_in.at[c],
            send_sem=rs_s.at[7, c], recv_sem=rs_r.at[7, c],
            device_id=to_sib, device_id_type=MESH,
        )

    def rs_got(kind, c):
        rs(kind, c, to_x).wait_recv()

    def total(c, goes, kinds):
        value = part[c, goes].astype(F32) + part_in[c, goes].astype(F32)
        for kind in kinds:
            value = value + land[kind, c].astype(F32)
        return value

    def rs_send(kind, c, there, kinds=()):
        leave[kind, c] = total(c, kind, kinds).astype(BF16)
        rs(kind, c, there).start()

    def rs_first(c):
        rs_pair(c).wait_recv()
        rs_send(A_UP, c, to_yp)
        rs_send(A_DN, c, to_ym)
        rs_send(C_UP, c, to_yp)
        rs_send(C_DN, c, to_ym)

    def rs_second(c):
        rs_got(A_UP, c)
        rs_send(E_UP, c, to_yp, (A_UP,))
        rs_got(A_DN, c)
        rs_send(F_DN, c, to_ym, (A_DN,))

    def rs_third(c):
        rs_got(C_UP, c)
        rs_got(F_DN, c)
        rs_send(G_X, c, to_x, (C_UP, F_DN))

    def rs_last(c):
        for kind in (C_DN, E_UP, G_X):
            rs_got(kind, c)
        value = total(c, MINE, (C_DN, E_UP, G_X)).astype(BF16)
        gg_ref[0, c] = value[0]
        gu_ref[0, c] = value[1]

    X_Y2, X_YP, X_YM, X_Y, TO_UP, TO_DN, HALF_DN = 1, 2, 5, 6, 4, 3, 8

    def rs_half(c, half):
        there, sem = ((to_yp, 0), (to_ym, HALF_DN))[half]
        return pltpu.make_async_remote_copy(
            src_ref=leave.at[0, c, half], dst_ref=land.at[0, c, half],
            send_sem=rs_s.at[sem, c], recv_sem=rs_r.at[sem, c],
            device_id=there, device_id_type=MESH,
        )

    def rs_first_odd(c):
        rs_pair(c).wait_recv()
        for kind in (X_Y2, X_YP, X_YM, X_Y):
            rs_send(kind, c, to_x)

    def rs_second_odd(c):
        rs_got(X_Y2, c)
        leave[0, c] = total(c, 0, (X_Y2,)).astype(BF16)
        rs_half(c, 0).start()
        rs_half(c, 1).start()

    def rs_third_odd(c):
        for kind, came, half, there in ((TO_UP, X_YP, 0, to_yp), (TO_DN, X_YM, 1, to_ym)):
            rs_got(came, c)
            value = total(c, kind, (came,))
            rs_half(c, half).wait_recv()
            leave[kind, c, half] = (value[half] + land[0, c, half].astype(F32)).astype(BF16)
            leave[kind, c, 1 - half] = value[1 - half].astype(BF16)
            rs(kind, c, there).start()

    def rs_last_odd(c):
        for kind in (X_Y, TO_UP, TO_DN):
            rs_got(kind, c)
        value = total(c, MINE, (X_Y, TO_UP, TO_DN)).astype(BF16)
        gg_ref[0, c] = value[0]
        gu_ref[0, c] = value[1]

    def rs_1(c):
        either(c, rs_first, rs_first_odd)

    def rs_2(c):
        either(c, rs_second, rs_second_odd)

    def rs_3(c):
        either(c, rs_third, rs_third_odd)

    def rs_4(c):
        either(c, rs_last, rs_last_odd)

    def weight(s, c):
        return jnp.concatenate([wbuf[s, c, 0], wbuf[s, c, 1]], axis=1)

    def compute(c):
        acc = jnp.zeros((B, 2 * B), F32)
        for s in range(0, KEEP, 2):
            lhs = jnp.concatenate([xbuf[rows[s, c]], xbuf[rows[s + 1, c]]], axis=1)
            rhs = jnp.concatenate([weight(s, c), weight(s + 1, c)], axis=0)
            acc = acc + jnp.dot(lhs, rhs, preferred_element_type=F32)
        gate, up = acc[:, :B], acc[:, B:]
        sig = jax.nn.sigmoid(gate)
        silu = gate * sig
        lanes = pl.ds(pl.multiple_of(c * B, B), B)
        hid_ref[:, lanes] = (silu * up).astype(BF16)
        grad = gh_ref[:, lanes].astype(F32)
        d_gate = (grad * up * sig * (1.0 + gate * (1.0 - sig))).astype(BF16)
        d_up = (grad * silu).astype(BF16)
        dt[c, :B] = d_gate.T
        dt[c, B:] = d_up.T
        delta = jnp.concatenate([d_gate, d_up], axis=1)
        for core, target in ((ko, part_out), (k, part)):
            for i in range(0, 8, 2):
                blocks = [xt[rows[slot(*goal[i + half], core), c]] for half in range(2)]
                lhs = jnp.concatenate(blocks, axis=0)
                out = (jnp.dot(lhs, delta, preferred_element_type=F32) * SCALE).astype(BF16)
                for half in range(2):
                    target[c, i + half, 0] = out[half * B : (half + 1) * B, :B]
                    target[c, i + half, 1] = out[half * B : (half + 1) * B, B:]
            if target is part_out:
                rs_pair(c).start()

    def column(c, _):
        @pl.when(c + 3 < NC)
        def _():
            either(c + 3, ag_fourth, ag_fourth_odd)

        ag_end(c)
        compute(c)

        @pl.when(c >= 1)
        def _():
            rs_1(c - 1)

        @pl.when(c >= 2)
        def _():
            rs_2(c - 2)

        @pl.when(c >= 3)
        def _():
            rs_3(c - 3)

        return 0

    lax.fori_loop(0, NC, column, 0)

    def unit(zz):
        def one(c, acc):
            lhs = jnp.concatenate([weight(rank[zz * 4 + b, c], c) for b in range(4)], axis=0)
            return acc + jnp.dot(lhs, dt[c], preferred_element_type=F32)

        return lax.fori_loop(0, NC, one, jnp.zeros((4 * B, B), F32)).reshape(4, B, B)

    def ring_copy(src, dst, sem, there):
        return pltpu.make_async_remote_copy(
            src_ref=src, dst_ref=dst, send_sem=dx_ss.at[sem], recv_sem=dx_rs.at[sem],
            device_id=there, device_id_type=MESH,
        )

    def go_up(n):
        cut = pl.ds(0, 2 if n == 0 else 4)
        return ring_copy(up_s.at[n, cut], up_r.at[n, cut], n, to_zp)

    def go_down(n):
        cut = pl.ds(2, 2) if n == 0 else pl.ds(0, 4)
        return ring_copy(dn_s.at[n, cut], dn_r.at[n, cut], 4 + n, to_zm)

    far = unit((z + 4) % 8).astype(BF16)
    up_s[0, :2] = far[:2]
    go_up(0).start()
    dn_s[0, 2:] = far[2:]
    go_down(0).start()

    def step(n):
        mine = unit((z + 4 - n) % 8)
        go_up(n - 1).wait_recv()
        if n == 1:
            up_s[n, :2] = (mine[:2] + up_r[0, :2].astype(F32)).astype(BF16)
            up_s[n, 2:] = mine[2:].astype(BF16)
        else:
            up_s[n] = (mine + up_r[n - 1].astype(F32)).astype(BF16)
        go_up(n).start()
        mine = unit((z + 4 + n) % 8)
        go_down(n - 1).wait_recv()
        if n == 1:
            dn_s[n, :2] = mine[:2].astype(BF16)
            dn_s[n, 2:] = (mine[2:] + dn_r[0, 2:].astype(F32)).astype(BF16)
        else:
            dn_s[n] = (mine + dn_r[n - 1].astype(F32)).astype(BF16)
        go_down(n).start()

    rs_1(6)
    rs_2(5)
    step(1)
    rs_2(6)
    rs_3(4)
    step(2)
    rs_3(5)
    rs_4(0)
    rs_4(1)
    step(3)
    rs_3(6)
    rs_4(2)
    rs_4(3)
    mine = unit(z)
    go_up(3).wait_recv()
    go_down(3).wait_recv()
    last_s[...] = (mine + up_r[3].astype(F32) + dn_r[3].astype(F32)).astype(BF16)
    across = ring_copy(last_s.at[pl.ds(ho * 2, 2)], last_r, 8, to_h)
    across.start()
    rs_4(4)
    rs_4(5)
    across.wait_recv()
    for b in range(2):
        value = last_s[h * 2 + b].astype(F32) + last_r[b].astype(F32)
        dx_ref[:, b * B : (b + 1) * B] = value.T.astype(BF16)

    rs_4(6)

    def sent(c, _):
        for kind in (1, 2, 3, 4, 5, 7, 8, 9, 10, 11, 12, 13, 14, 15):
            ag(kind, 0, c, to_x, k).wait_send()
        for kind in range(1, 7):
            rs(kind, c, to_x).wait_send()
        rs_pair(c).wait_send()
        either(c, sent_even, sent_odd)
        return 0

    def sent_even(c):
        ag(P2, 0, c, to_x, k).wait_send()
        rs(0, c, to_x).wait_send()

    def sent_odd(c):
        ag_half(P2, 0, c, 0, to_yp).wait_send()
        ag_half(HALF, 0, c, 1, to_ym).wait_send()
        rs_half(c, 0).wait_send()
        rs_half(c, 1).wait_send()

    lax.fori_loop(0, NC, sent, 0)
    for sem in range(15):
        inp(sem, z, h, to_h).wait_send()
    for n in range(4):
        go_up(n).wait_send()
        go_down(n).wait_send()
    across.wait_send()


def per_device(inputs, gate_blocks, up_blocks, block_mask, grad_hidden):
    vmem = pl.BlockSpec(memory_space=pltpu.VMEM)
    dma = pltpu.SemaphoreType.DMA
    unit = (4, B, B)
    return pl.pallas_call(
        kernel,
        out_shape=(
            jax.ShapeDtypeStruct(grad_hidden.shape, BF16),
            jax.ShapeDtypeStruct(inputs.shape, BF16),
            jax.ShapeDtypeStruct(gate_blocks.shape, BF16),
            jax.ShapeDtypeStruct(up_blocks.shape, BF16),
        ),
        in_specs=[vmem, vmem, vmem, pl.BlockSpec(memory_space=pltpu.SMEM), vmem],
        out_specs=(vmem, vmem, vmem, vmem),
        scratch_shapes=[
            pltpu.VMEM((KEEP + 1, NC, 2, B, B), BF16),
            pltpu.VMEM((RB, B, B), BF16),
            pltpu.VMEM((RB, B, B), BF16),
            pltpu.VMEM((NC, 2 * B, B), BF16),
            pltpu.VMEM((NC, 8, 2, B, B), BF16),
            pltpu.VMEM((NC, 8, 2, B, B), BF16),
            pltpu.VMEM((NC, 8, 2, B, B), BF16),
            pltpu.VMEM((7, NC, 2, B, B), BF16),
            pltpu.VMEM((7, NC, 2, B, B), BF16),
            pltpu.VMEM((4,) + unit, BF16),
            pltpu.VMEM((4,) + unit, BF16),
            pltpu.VMEM((4,) + unit, BF16),
            pltpu.VMEM((4,) + unit, BF16),
            pltpu.VMEM(unit, BF16),
            pltpu.VMEM((2, B, B), BF16),
            pltpu.SMEM((RB, NC), jnp.int32),
            pltpu.SMEM((KEEP, NC), jnp.int32),
            pltpu.SMEM((RB,), jnp.int32),
            dma((16, NC)),
            dma((16, NC)),
            dma((15,)),
            dma((15,)),
            dma((9, NC)),
            dma((9, NC)),
            dma((9,)),
            dma((9,)),
        ],
        compiler_params=pltpu.CompilerParams(
            collective_id=0, has_side_effects=True, vmem_limit_bytes=56 * 2**20
        ),
        cost_estimate=pl.CostEstimate(
            flops=4 * 10**9, bytes_accessed=3 * 2**20, transcendentals=128 * 896
        ),
    )(inputs, gate_blocks, up_blocks, block_mask, grad_hidden)


def solution(mesh):
    return jax.shard_map(
        per_device,
        mesh=mesh,
        in_specs=(
            P("dp", "tensor"),
            P("dp", "tensor", None, None),
            P("dp", "tensor", None, None),
            P(None, "tensor"),
            P("dp", "tensor"),
        ),
        out_specs=(
            P("dp", "tensor"),
            P("dp", "tensor"),
            P("dp", "tensor", None, None),
            P("dp", "tensor", None, None),
        ),
        check_vma=False,
    )
```

```python
import jax
import jax.numpy as jnp
from jax import lax
from jax.experimental import pallas as pl
from jax.experimental.pallas import tpu as pltpu
from jax.sharding import PartitionSpec as P

MESH = pl.DeviceIdType.MESH
F32, BF16 = jnp.float32, jnp.bfloat16
B = 128
NC = 7
KEEP = 16
RB = 32
SCALE = 2048.0**-0.5


def kernel(
    x_ref, g_ref, u_ref, mask_ref, gh_ref,
    hid_ref, dx_ref, gg_ref, gu_ref,
    wbuf, xbuf, xt, dt, part_out, part_in, part, leave, land, up_s, up_r, dn_s, dn_r, last_s, last_r,
    rank, rows, following,
    ag_s, ag_r, in_s, in_r, rs_s, rs_r, dx_ss, dx_rs,
):
    dp, tn = lax.axis_index("dp"), lax.axis_index("tensor")
    y, x, k = dp // 4, (dp // 2) % 2, dp % 2
    z, h = tn // 2, tn % 2
    yp, ym, y2 = (y + 1) % 4, (y + 3) % 4, (y + 2) % 4
    zp, zm = (z + 1) % 8, (z + 7) % 8
    xo, ko, ho = 1 - x, 1 - k, 1 - h

    def slot(yy, xx, kk):
        return yy * 4 + xx * 2 + kk

    to_sib = (slot(y, x, ko), tn)
    to_x = (slot(y, xo, k), tn)
    to_yp = (slot(yp, x, k), tn)
    to_ym = (slot(ym, x, k), tn)
    to_zp = (dp, zp * 2 + h)
    to_zm = (dp, zm * 2 + h)
    to_h = (dp, z * 2 + ho)
    neighbours = (to_sib, to_x, to_yp, to_ym, to_zp, to_zm, to_h)

    barrier = pltpu.get_barrier_semaphore()
    for there in neighbours:
        pl.semaphore_signal(barrier, inc=1, device_id=there, device_id_type=MESH)

    for c in range(NC):
        wbuf[dp, c, 0] = g_ref[0, c]
        wbuf[dp, c, 1] = u_ref[0, c]
        wbuf[KEEP, c] = jnp.zeros((2, B, B), BF16)
    for b in range(2):
        xbuf[tn * 2 + b] = x_ref[:, b * B : (b + 1) * B]
    pl.semaphore_wait(barrier, len(neighbours))

    ring = ((y, x), (y, xo), (ym, x), (yp, x), (ym, xo), (yp, xo), (y2, x), (y2, xo))
    OWN, N, PP, MM, NP, NM, P2, M2 = range(8)

    def ag(kind, which, c, there, core):
        s = slot(*ring[which], core)
        return pltpu.make_async_remote_copy(
            src_ref=wbuf.at[s, c], dst_ref=wbuf.at[s, c],
            send_sem=ag_s.at[c], recv_sem=ag_r.at[min(kind, 8), c],
            device_id=there, device_id_type=MESH,
        )

    def ag_send(kind, which, c, there):
        ag(kind, which, c, there, k).start()

    def ag_got(kind, c):
        ag(kind, kind, c, to_x, k).wait_recv()

    def ag_share(which, c):
        ag(8 + which, which, c, to_sib, k).start()

    def ag_own(c):
        ag_send(N, OWN, c, to_x)
        ag_send(PP, OWN, c, to_yp)
        ag_send(MM, OWN, c, to_ym)
        ag_share(OWN, c)

    def ag_second(c):
        ag_got(N, c)
        ag_send(NP, N, c, to_yp)
        ag_send(NM, N, c, to_ym)
        ag_share(N, c)

    def ag_third(c):
        ag_got(PP, c)
        ag_send(P2, PP, c, to_yp)
        ag_share(PP, c)
        ag_got(MM, c)
        ag_share(MM, c)
        ag_got(NM, c)
        ag_send(M2, NM, c, to_ym)
        ag_share(NM, c)
        ag_got(NP, c)
        ag_share(NP, c)

    def ag_fourth(c):
        ag_got(P2, c)
        ag_share(P2, c)
        ag_got(M2, c)
        ag_share(M2, c)

    HALF = 0

    def ag_half(kind, which, c, half, there):
        s = slot(*ring[which], k)
        return pltpu.make_async_remote_copy(
            src_ref=wbuf.at[s, c, half], dst_ref=wbuf.at[s, c, half],
            send_sem=ag_s.at[c], recv_sem=ag_r.at[kind, c],
            device_id=there, device_id_type=MESH,
        )

    def ag_second_odd(c):
        ag_got(PP, c)
        ag_half(P2, PP, c, 0, to_yp).start()
        ag_send(NP, PP, c, to_x)
        ag_share(PP, c)
        ag_got(MM, c)
        ag_half(HALF, MM, c, 1, to_ym).start()
        ag_send(NM, MM, c, to_x)
        ag_share(MM, c)
        ag_got(N, c)
        ag_share(N, c)

    def ag_third_odd(c):
        ag_half(P2, P2, c, 0, to_yp).wait_recv()
        ag_half(HALF, P2, c, 1, to_ym).wait_recv()
        ag_send(M2, P2, c, to_x)
        ag_share(P2, c)
        ag_got(NP, c)
        ag_share(NP, c)
        ag_got(NM, c)
        ag_share(NM, c)

    def ag_fourth_odd(c):
        ag_got(M2, c)
        ag_share(M2, c)

    def either(c, even, odd):
        if isinstance(c, int):
            (odd if c % 2 else even)(c)
        else:
            pl.when(c % 2 == 0)(lambda: even(c))
            pl.when(c % 2 == 1)(lambda: odd(c))

    def ag_end(c):
        pltpu.make_async_remote_copy(
            src_ref=part_in.at[c], dst_ref=part_in.at[c],
            send_sem=ag_s.at[c], recv_sem=ag_r.at[8, c],
            device_id=to_sib, device_id_type=MESH,
        ).wait_recv()

    def inp(sem, zz, hh, there):
        at = pl.ds(((zz + 8) % 8) * 4 + hh * 2, 2)
        return pltpu.make_async_remote_copy(
            src_ref=xbuf.at[at], dst_ref=xbuf.at[at],
            send_sem=in_s.at[0], recv_sem=in_r.at[sem],
            device_id=there, device_id_type=MESH,
        )

    own_up, oth_dn, own_dn, oth_up = 0, 4, 8, 11

    inp(0, z, h, to_h).start()
    inp(own_up + 1, z, h, to_zp).start()
    inp(own_dn + 1, z, h, to_zm).start()
    for c in range(NC):
        ag_own(c)

    inp(0, z, ho, to_h).wait_recv()
    inp(oth_up + 1, z, ho, to_zp).start()
    inp(oth_dn + 1, z, ho, to_zm).start()

    def column_tables(c, _):
        def count(r, seen):
            here = mask_ref[r, c]
            rank[r, c] = jnp.where(here == 1, jnp.minimum(seen, KEEP - 1), KEEP)
            return seen + here

        lax.fori_loop(0, RB, count, jnp.int32(0))

        def back(q, after):
            r = RB - 1 - q
            after = jnp.where(mask_ref[r, c] == 1, r, after)
            following[r] = after
            return after

        lax.fori_loop(0, RB, back, jnp.int32(RB - 1))

        def pick(kk, r):
            r = following[jnp.minimum(r, RB - 1)]
            rows[kk, c] = r
            return r + 1

        lax.fori_loop(0, KEEP, pick, jnp.int32(0))
        return 0

    lax.fori_loop(0, NC, column_tables, 0)

    for j in (1, 2, 3, 4):
        inp(own_up + j, z - j, h, to_zp).wait_recv()
        if j < 4:
            inp(own_up + j + 1, z - j, h, to_zp).start()
        if j < 4:
            inp(own_dn + j, z + j, h, to_zm).wait_recv()
            if j < 3:
                inp(own_dn + j + 1, z + j, h, to_zm).start()
            inp(oth_up + j, z - j, ho, to_zp).wait_recv()
            if j < 3:
                inp(oth_up + j + 1, z - j, ho, to_zp).start()
        inp(oth_dn + j, z + j, ho, to_zm).wait_recv()
        if j < 4:
            inp(oth_dn + j + 1, z + j, ho, to_zm).start()
        for c in ((), (0, 1, 2), (3, 4, 5, 6), (), ())[j]:
            either(c, ag_second, ag_second_odd)
        for c in ((), (), (0,), (1, 2, 3), (4, 5))[j]:
            either(c, ag_third, ag_third_odd)
        for c in ((), (), (), (0,), (1,))[j]:
            either(c, ag_fourth, ag_fourth_odd)

    def turn(r, _):
        xt[r] = xbuf[r].T
        return 0

    lax.fori_loop(0, RB, turn, 0)
    ag_third(6)
    ag_fourth(2)

    A_UP, A_DN, C_UP, C_DN, E_UP, F_DN, G_X = range(7)

    goal = ((y2, x), (y2, xo), (yp, xo), (ym, x), (yp, x), (ym, xo), (y, xo), (y, x))
    MINE = 7

    def rs(kind, c, there):
        return pltpu.make_async_remote_copy(
            src_ref=leave.at[kind, c], dst_ref=land.at[kind, c],
            send_sem=rs_s.at[c], recv_sem=rs_r.at[kind, c],
            device_id=there, device_id_type=MESH,
        )

    def rs_pair(c):
        return pltpu.make_async_remote_copy(
            src_ref=part_out.at[c], dst_ref=part_in.at[c],
            send_sem=rs_s.at[c], recv_sem=rs_r.at[7, c],
            device_id=to_sib, device_id_type=MESH,
        )

    def rs_got(kind, c):
        rs(kind, c, to_x).wait_recv()

    def total(c, goes, kinds):
        value = part[c, goes].astype(F32) + part_in[c, goes].astype(F32)
        for kind in kinds:
            value = value + land[kind, c].astype(F32)
        return value

    def rs_send(kind, c, there, kinds=()):
        leave[kind, c] = total(c, kind, kinds).astype(BF16)
        rs(kind, c, there).start()

    def rs_first(c):
        rs_pair(c).wait_recv()
        rs_send(A_UP, c, to_yp)
        rs_send(A_DN, c, to_ym)
        rs_send(C_UP, c, to_yp)
        rs_send(C_DN, c, to_ym)

    def rs_second(c):
        rs_got(A_UP, c)
        rs_send(E_UP, c, to_yp, (A_UP,))
        rs_got(A_DN, c)
        rs_send(F_DN, c, to_ym, (A_DN,))

    def rs_third(c):
        rs_got(C_UP, c)
        rs_got(F_DN, c)
        rs_send(G_X, c, to_x, (C_UP, F_DN))

    def rs_last(c):
        for kind in (C_DN, E_UP, G_X):
            rs_got(kind, c)
        value = total(c, MINE, (C_DN, E_UP, G_X)).astype(BF16)
        gg_ref[0, c] = value[0]
        gu_ref[0, c] = value[1]

    X_Y2, X_YP, X_YM, X_Y, TO_UP, TO_DN, HALF_DN = 1, 2, 5, 6, 4, 3, 8

    def rs_half(c, half):
        there, sem = ((to_yp, 0), (to_ym, HALF_DN))[half]
        return pltpu.make_async_remote_copy(
            src_ref=leave.at[0, c, half], dst_ref=land.at[0, c, half],
            send_sem=rs_s.at[c], recv_sem=rs_r.at[sem, c],
            device_id=there, device_id_type=MESH,
        )

    def rs_first_odd(c):
        rs_pair(c).wait_recv()
        for kind in (X_Y2, X_YP, X_YM, X_Y):
            rs_send(kind, c, to_x)

    def rs_second_odd(c):
        rs_got(X_Y2, c)
        leave[0, c] = total(c, 0, (X_Y2,)).astype(BF16)
        rs_half(c, 0).start()
        rs_half(c, 1).start()

    def rs_third_odd(c):
        for kind, came, half, there in ((TO_UP, X_YP, 0, to_yp), (TO_DN, X_YM, 1, to_ym)):
            rs_got(came, c)
            value = total(c, kind, (came,))
            rs_half(c, half).wait_recv()
            leave[kind, c, half] = (value[half] + land[0, c, half].astype(F32)).astype(BF16)
            leave[kind, c, 1 - half] = value[1 - half].astype(BF16)
            rs(kind, c, there).start()

    def rs_last_odd(c):
        for kind in (X_Y, TO_UP, TO_DN):
            rs_got(kind, c)
        value = total(c, MINE, (X_Y, TO_UP, TO_DN)).astype(BF16)
        gg_ref[0, c] = value[0]
        gu_ref[0, c] = value[1]

    def rs_1(c):
        either(c, rs_first, rs_first_odd)

    def rs_2(c):
        either(c, rs_second, rs_second_odd)

    def rs_3(c):
        either(c, rs_third, rs_third_odd)

    def rs_4(c):
        either(c, rs_last, rs_last_odd)

    def weight(s, c):
        return jnp.concatenate([wbuf[s, c, 0], wbuf[s, c, 1]], axis=1)

    def compute(c):
        acc = jnp.zeros((B, 2 * B), F32)
        for s in range(0, KEEP, 2):
            lhs = jnp.concatenate([xbuf[rows[s, c]], xbuf[rows[s + 1, c]]], axis=1)
            rhs = jnp.concatenate([weight(s, c), weight(s + 1, c)], axis=0)
            acc = acc + jnp.dot(lhs, rhs, preferred_element_type=F32)
        gate, up = acc[:, :B], acc[:, B:]
        sig = jax.nn.sigmoid(gate)
        silu = gate * sig
        lanes = pl.ds(pl.multiple_of(c * B, B), B)
        hid_ref[:, lanes] = (silu * up).astype(BF16)
        grad = gh_ref[:, lanes].astype(F32)
        d_gate = (grad * up * sig * (1.0 + gate * (1.0 - sig))).astype(BF16)
        d_up = (grad * silu).astype(BF16)
        dt[c, :B] = d_gate.T
        dt[c, B:] = d_up.T
        delta = jnp.concatenate([d_gate, d_up], axis=1)
        for core, target in ((ko, part_out), (k, part)):
            for i in range(0, 8, 2):
                blocks = [xt[rows[slot(*goal[i + half], core), c]] for half in range(2)]
                lhs = jnp.concatenate(blocks, axis=0)
                out = (jnp.dot(lhs, delta, preferred_element_type=F32) * SCALE).astype(BF16)
                for half in range(2):
                    target[c, i + half, 0] = out[half * B : (half + 1) * B, :B]
                    target[c, i + half, 1] = out[half * B : (half + 1) * B, B:]
            if target is part_out:
                rs_pair(c).start()

    def column(c, _):
        @pl.when(c + 3 < NC)
        def _():
            either(c + 3, ag_fourth, ag_fourth_odd)

        ag_end(c)
        compute(c)

        @pl.when(c >= 1)
        def _():
            rs_1(c - 1)

        @pl.when(c >= 2)
        def _():
            rs_2(c - 2)

        @pl.when(c >= 3)
        def _():
            rs_3(c - 3)

        return 0

    lax.fori_loop(0, NC, column, 0)

    def unit(zz):
        def one(c, acc):
            lhs = jnp.concatenate([weight(rank[zz * 4 + b, c], c) for b in range(4)], axis=0)
            return acc + jnp.dot(lhs, dt[c], preferred_element_type=F32)

        return lax.fori_loop(0, NC, one, jnp.zeros((4 * B, B), F32)).reshape(4, B, B)

    def ring_copy(src, dst, sem, there):
        return pltpu.make_async_remote_copy(
            src_ref=src, dst_ref=dst, send_sem=dx_ss.at[0], recv_sem=dx_rs.at[sem],
            device_id=there, device_id_type=MESH,
        )

    def go_up(n, half):
        cut = pl.ds(2 * half, 2)
        return ring_copy(up_s.at[n, cut], up_r.at[n, cut], 2 * n + half, to_zp)

    def go_down(n, half):
        cut = pl.ds(2 * half, 2)
        return ring_copy(dn_s.at[n, cut], dn_r.at[n, cut], 8 + 2 * n + half, to_zm)

    far = unit((z + 4) % 8).astype(BF16)
    up_s[0, :2] = far[:2]
    go_up(0, 0).start()
    dn_s[0, 2:] = far[2:]
    go_down(0, 1).start()

    def pass_on(n, go, out, came, mine, order):
        for half in order:
            cut = slice(2 * half, 2 * half + 2)
            value = mine[cut]
            if n > 1 or half == order[1]:
                go(n - 1, half).wait_recv()
                value = value + came[n - 1, cut].astype(F32)
            out[n, cut] = value.astype(BF16)
            go(n, half).start()

    def step(n):
        pass_on(n, go_up, up_s, up_r, unit((z + 4 - n) % 8), (1, 0))
        pass_on(n, go_down, dn_s, dn_r, unit((z + 4 + n) % 8), (0, 1))

    rs_1(6)
    rs_2(5)
    step(1)
    rs_2(6)
    rs_3(4)
    step(2)
    rs_3(5)
    rs_4(0)
    rs_4(1)
    step(3)
    rs_3(6)
    rs_4(2)
    rs_4(3)
    mine = unit(z)
    for half in range(2):
        go_up(3, half).wait_recv()
        go_down(3, half).wait_recv()
    last_s[...] = (mine + up_r[3].astype(F32) + dn_r[3].astype(F32)).astype(BF16)
    across = ring_copy(last_s.at[pl.ds(ho * 2, 2)], last_r, 16, to_h)
    across.start()
    rs_4(4)
    rs_4(5)
    across.wait_recv()
    for b in range(2):
        value = last_s[h * 2 + b].astype(F32) + last_r[b].astype(F32)
        dx_ref[:, b * B : (b + 1) * B] = value.T.astype(BF16)

    rs_4(6)

    def sent(sem):
        pltpu.make_async_remote_copy(
            src_ref=xbuf.at[pl.ds(0, 30)], dst_ref=xbuf.at[pl.ds(0, 30)],
            send_sem=sem, recv_sem=in_r.at[0],
            device_id=to_h, device_id_type=MESH,
        ).wait_send()

    def column_sent(c, _):
        sent(ag_s.at[c])
        sent(rs_s.at[c])
        return 0

    lax.fori_loop(0, NC, column_sent, 0)
    sent(in_s.at[0])
    sent(dx_ss.at[0])


def per_device(inputs, gate_blocks, up_blocks, block_mask, grad_hidden):
    vmem = pl.BlockSpec(memory_space=pltpu.VMEM)
    dma = pltpu.SemaphoreType.DMA
    unit = (4, B, B)
    return pl.pallas_call(
        kernel,
        out_shape=(
            jax.ShapeDtypeStruct(grad_hidden.shape, BF16),
            jax.ShapeDtypeStruct(inputs.shape, BF16),
            jax.ShapeDtypeStruct(gate_blocks.shape, BF16),
            jax.ShapeDtypeStruct(up_blocks.shape, BF16),
        ),
        in_specs=[vmem, vmem, vmem, pl.BlockSpec(memory_space=pltpu.SMEM), vmem],
        out_specs=(vmem, vmem, vmem, vmem),
        scratch_shapes=[
            pltpu.VMEM((KEEP + 1, NC, 2, B, B), BF16),
            pltpu.VMEM((RB, B, B), BF16),
            pltpu.VMEM((RB, B, B), BF16),
            pltpu.VMEM((NC, 2 * B, B), BF16),
            pltpu.VMEM((NC, 8, 2, B, B), BF16),
            pltpu.VMEM((NC, 8, 2, B, B), BF16),
            pltpu.VMEM((NC, 8, 2, B, B), BF16),
            pltpu.VMEM((7, NC, 2, B, B), BF16),
            pltpu.VMEM((7, NC, 2, B, B), BF16),
            pltpu.VMEM((4,) + unit, BF16),
            pltpu.VMEM((4,) + unit, BF16),
            pltpu.VMEM((4,) + unit, BF16),
            pltpu.VMEM((4,) + unit, BF16),
            pltpu.VMEM(unit, BF16),
            pltpu.VMEM((2, B, B), BF16),
            pltpu.SMEM((RB, NC), jnp.int32),
            pltpu.SMEM((KEEP, NC), jnp.int32),
            pltpu.SMEM((RB,), jnp.int32),
            dma((NC,)),
            dma((9, NC)),
            dma((1,)),
            dma((15,)),
            dma((NC,)),
            dma((9, NC)),
            dma((1,)),
            dma((17,)),
        ],
        compiler_params=pltpu.CompilerParams(
            collective_id=0, has_side_effects=True, vmem_limit_bytes=56 * 2**20
        ),
        cost_estimate=pl.CostEstimate(
            flops=4 * 10**9, bytes_accessed=3 * 2**20, transcendentals=128 * 896
        ),
    )(inputs, gate_blocks, up_blocks, block_mask, grad_hidden)


def solution(mesh):
    return jax.shard_map(
        per_device,
        mesh=mesh,
        in_specs=(
            P("dp", "tensor"),
            P("dp", "tensor", None, None),
            P("dp", "tensor", None, None),
            P(None, "tensor"),
            P("dp", "tensor"),
        ),
        out_specs=(
            P("dp", "tensor"),
            P("dp", "tensor"),
            P("dp", "tensor", None, None),
            P("dp", "tensor", None, None),
        ),
        check_vma=False,
    )
```

```python
import jax
import jax.numpy as jnp
from jax import lax
from jax.experimental import pallas as pl
from jax.experimental.pallas import tpu as pltpu
from jax.sharding import PartitionSpec as P

MESH = pl.DeviceIdType.MESH
F32, BF16 = jnp.float32, jnp.bfloat16
B = 128
NC = 7
KEEP = 16
RB = 32
SCALE = 2048.0**-0.5


def kernel(
    x_ref, g_ref, u_ref, mask_ref, gh_ref,
    hid_ref, dx_ref, gg_ref, gu_ref,
    wbuf, xbuf, xt, dt, part_out, part_in, part, leave, land, up_s, up_r, dn_s, dn_r, last_s, last_r,
    rank, rows, following,
    ag_s, ag_r, in_s, in_r, rs_s, rs_r, dx_ss, dx_rs,
):
    dp, tn = lax.axis_index("dp"), lax.axis_index("tensor")
    y, x, k = dp // 4, (dp // 2) % 2, dp % 2
    z, h = tn // 2, tn % 2
    yp, ym, y2 = (y + 1) % 4, (y + 3) % 4, (y + 2) % 4
    zp, zm = (z + 1) % 8, (z + 7) % 8
    xo, ko, ho = 1 - x, 1 - k, 1 - h

    def slot(yy, xx, kk):
        return yy * 4 + xx * 2 + kk

    to_sib = (slot(y, x, ko), tn)
    to_x = (slot(y, xo, k), tn)
    to_yp = (slot(yp, x, k), tn)
    to_ym = (slot(ym, x, k), tn)
    to_zp = (dp, zp * 2 + h)
    to_zm = (dp, zm * 2 + h)
    to_h = (dp, z * 2 + ho)
    neighbours = (to_sib, to_x, to_yp, to_ym, to_zp, to_zm, to_h)

    barrier = pltpu.get_barrier_semaphore()
    for there in neighbours:
        pl.semaphore_signal(barrier, inc=1, device_id=there, device_id_type=MESH)

    for c in range(NC):
        wbuf[dp, c, 0] = g_ref[0, c]
        wbuf[dp, c, 1] = u_ref[0, c]
        wbuf[KEEP, c] = jnp.zeros((2, B, B), BF16)
    for b in range(2):
        xbuf[tn * 2 + b] = x_ref[:, b * B : (b + 1) * B]
    pl.semaphore_wait(barrier, len(neighbours))

    ring = ((y, x), (y, xo), (ym, x), (yp, x), (ym, xo), (yp, xo), (y2, x), (y2, xo))
    OWN, N, PP, MM, NP, NM, P2, M2 = range(8)

    def ag(kind, which, c, there, core):
        s = slot(*ring[which], core)
        return pltpu.make_async_remote_copy(
            src_ref=wbuf.at[s, c], dst_ref=wbuf.at[s, c],
            send_sem=ag_s.at[c], recv_sem=ag_r.at[min(kind, 8), c],
            device_id=there, device_id_type=MESH,
        )

    def ag_send(kind, which, c, there):
        ag(kind, which, c, there, k).start()

    def ag_got(kind, c):
        ag(kind, kind, c, to_x, k).wait_recv()

    def ag_share(which, c):
        ag(8 + which, which, c, to_sib, k).start()

    def ag_own(c):
        ag_send(N, OWN, c, to_x)
        ag_send(PP, OWN, c, to_yp)
        ag_send(MM, OWN, c, to_ym)
        ag_share(OWN, c)

    def ag_second(c):
        ag_got(N, c)
        ag_send(NP, N, c, to_yp)
        ag_send(NM, N, c, to_ym)
        ag_share(N, c)

    def ag_third(c):
        ag_got(PP, c)
        ag_send(P2, PP, c, to_yp)
        ag_share(PP, c)
        ag_got(MM, c)
        ag_share(MM, c)
        ag_got(NM, c)
        ag_send(M2, NM, c, to_ym)
        ag_share(NM, c)
        ag_got(NP, c)
        ag_share(NP, c)

    def ag_fourth(c):
        ag_got(P2, c)
        ag_share(P2, c)
        ag_got(M2, c)
        ag_share(M2, c)

    HALF = 0

    def ag_half(kind, which, c, half, there):
        s = slot(*ring[which], k)
        return pltpu.make_async_remote_copy(
            src_ref=wbuf.at[s, c, half], dst_ref=wbuf.at[s, c, half],
            send_sem=ag_s.at[c], recv_sem=ag_r.at[kind, c],
            device_id=there, device_id_type=MESH,
        )

    def ag_second_odd(c):
        ag_got(PP, c)
        ag_half(P2, PP, c, 0, to_yp).start()
        ag_send(NP, PP, c, to_x)
        ag_share(PP, c)
        ag_got(MM, c)
        ag_half(HALF, MM, c, 1, to_ym).start()
        ag_send(NM, MM, c, to_x)
        ag_share(MM, c)
        ag_got(N, c)
        ag_share(N, c)

    def ag_third_odd(c):
        ag_half(P2, P2, c, 0, to_yp).wait_recv()
        ag_half(HALF, P2, c, 1, to_ym).wait_recv()
        ag_send(M2, P2, c, to_x)
        ag_share(P2, c)
        ag_got(NP, c)
        ag_share(NP, c)
        ag_got(NM, c)
        ag_share(NM, c)

    def ag_fourth_odd(c):
        ag_got(M2, c)
        ag_share(M2, c)

    def either(c, even, odd):
        if isinstance(c, int):
            (odd if c % 2 else even)(c)
        else:
            pl.when(c % 2 == 0)(lambda: even(c))
            pl.when(c % 2 == 1)(lambda: odd(c))

    def ag_end(c):
        pltpu.make_async_remote_copy(
            src_ref=part_in.at[c], dst_ref=part_in.at[c],
            send_sem=ag_s.at[c], recv_sem=ag_r.at[8, c],
            device_id=to_sib, device_id_type=MESH,
        ).wait_recv()

    def inp(sem, zz, hh, there):
        at = pl.ds(((zz + 8) % 8) * 4 + hh * 2, 2)
        return pltpu.make_async_remote_copy(
            src_ref=xbuf.at[at], dst_ref=xbuf.at[at],
            send_sem=in_s.at[0], recv_sem=in_r.at[sem],
            device_id=there, device_id_type=MESH,
        )

    own_up, oth_dn, own_dn, oth_up = 0, 4, 8, 11

    inp(0, z, h, to_h).start()
    inp(own_up + 1, z, h, to_zp).start()
    inp(own_dn + 1, z, h, to_zm).start()
    for c in range(NC):
        ag_own(c)

    inp(0, z, ho, to_h).wait_recv()
    inp(oth_up + 1, z, ho, to_zp).start()
    inp(oth_dn + 1, z, ho, to_zm).start()

    def column_tables(c, _):
        def count(r, seen):
            here = mask_ref[r, c]
            rank[r, c] = jnp.where(here == 1, jnp.minimum(seen, KEEP - 1), KEEP)
            return seen + here

        lax.fori_loop(0, RB, count, jnp.int32(0))

        def back(q, after):
            r = RB - 1 - q
            after = jnp.where(mask_ref[r, c] == 1, r, after)
            following[r] = after
            return after

        lax.fori_loop(0, RB, back, jnp.int32(RB - 1))

        def pick(kk, r):
            r = following[jnp.minimum(r, RB - 1)]
            rows[kk, c] = r
            return r + 1

        lax.fori_loop(0, KEEP, pick, jnp.int32(0))
        return 0

    lax.fori_loop(0, NC, column_tables, 0)

    for j in (1, 2, 3, 4):
        inp(own_up + j, z - j, h, to_zp).wait_recv()
        if j < 4:
            inp(own_up + j + 1, z - j, h, to_zp).start()
        if j < 4:
            inp(own_dn + j, z + j, h, to_zm).wait_recv()
            if j < 3:
                inp(own_dn + j + 1, z + j, h, to_zm).start()
            inp(oth_up + j, z - j, ho, to_zp).wait_recv()
            if j < 3:
                inp(oth_up + j + 1, z - j, ho, to_zp).start()
        inp(oth_dn + j, z + j, ho, to_zm).wait_recv()
        if j < 4:
            inp(oth_dn + j + 1, z + j, ho, to_zm).start()
        for c in ((), (0, 1, 2), (3, 4, 5, 6), (), ())[j]:
            either(c, ag_second, ag_second_odd)
        for c in ((), (), (0,), (1, 2, 3), (4, 5))[j]:
            either(c, ag_third, ag_third_odd)
        for c in ((), (), (), (0,), (1,))[j]:
            either(c, ag_fourth, ag_fourth_odd)

    def turn(r, _):
        xt[r] = xbuf[r].T
        return 0

    lax.fori_loop(0, RB, turn, 0)
    ag_third(6)
    ag_fourth(2)

    A_UP, A_DN, C_UP, C_DN, E_UP, F_DN, G_X = range(7)

    goal = ((y2, x), (y2, xo), (yp, xo), (ym, x), (yp, x), (ym, xo), (y, xo), (y, x))
    MINE = 7

    def rs(kind, c, there):
        return pltpu.make_async_remote_copy(
            src_ref=leave.at[kind, c], dst_ref=land.at[kind, c],
            send_sem=rs_s.at[c], recv_sem=rs_r.at[kind, c],
            device_id=there, device_id_type=MESH,
        )

    def rs_pair(c):
        return pltpu.make_async_remote_copy(
            src_ref=part_out.at[c], dst_ref=part_in.at[c],
            send_sem=rs_s.at[c], recv_sem=rs_r.at[7, c],
            device_id=to_sib, device_id_type=MESH,
        )

    def rs_got(kind, c):
        rs(kind, c, to_x).wait_recv()

    def total(c, goes, kinds):
        value = part[c, goes].astype(F32) + part_in[c, goes].astype(F32)
        for kind in kinds:
            value = value + land[kind, c].astype(F32)
        return value

    def rs_send(kind, c, there, kinds=()):
        leave[kind, c] = total(c, kind, kinds).astype(BF16)
        rs(kind, c, there).start()

    def rs_first(c):
        rs_pair(c).wait_recv()
        rs_send(A_UP, c, to_yp)
        rs_send(A_DN, c, to_ym)
        rs_send(C_UP, c, to_yp)
        rs_send(C_DN, c, to_ym)

    def rs_second(c):
        rs_got(A_UP, c)
        rs_send(E_UP, c, to_yp, (A_UP,))
        rs_got(A_DN, c)
        rs_send(F_DN, c, to_ym, (A_DN,))

    def rs_third(c):
        rs_got(C_UP, c)
        rs_got(F_DN, c)
        rs_send(G_X, c, to_x, (C_UP, F_DN))

    def rs_last(c):
        for kind in (C_DN, E_UP, G_X):
            rs_got(kind, c)
        value = total(c, MINE, (C_DN, E_UP, G_X)).astype(BF16)
        gg_ref[0, c] = value[0]
        gu_ref[0, c] = value[1]

    X_Y2, X_YP, X_YM, X_Y, TO_UP, TO_DN, HALF_DN = 1, 2, 5, 6, 4, 3, 8

    def rs_half(c, half):
        there, sem = ((to_yp, 0), (to_ym, HALF_DN))[half]
        return pltpu.make_async_remote_copy(
            src_ref=leave.at[0, c, half], dst_ref=land.at[0, c, half],
            send_sem=rs_s.at[c], recv_sem=rs_r.at[sem, c],
            device_id=there, device_id_type=MESH,
        )

    def rs_first_odd(c):
        rs_pair(c).wait_recv()
        for kind in (X_Y2, X_YP, X_YM, X_Y):
            rs_send(kind, c, to_x)

    def rs_second_odd(c):
        rs_got(X_Y2, c)
        leave[0, c] = total(c, 0, (X_Y2,)).astype(BF16)
        rs_half(c, 0).start()
        rs_half(c, 1).start()

    def rs_third_odd(c):
        for kind, came, half, there in ((TO_UP, X_YP, 0, to_yp), (TO_DN, X_YM, 1, to_ym)):
            rs_got(came, c)
            value = total(c, kind, (came,))
            rs_half(c, half).wait_recv()
            leave[kind, c, half] = (value[half] + land[0, c, half].astype(F32)).astype(BF16)
            leave[kind, c, 1 - half] = value[1 - half].astype(BF16)
            rs(kind, c, there).start()

    def rs_last_odd(c):
        for kind in (X_Y, TO_UP, TO_DN):
            rs_got(kind, c)
        value = total(c, MINE, (X_Y, TO_UP, TO_DN)).astype(BF16)
        gg_ref[0, c] = value[0]
        gu_ref[0, c] = value[1]

    def rs_1(c):
        either(c, rs_first, rs_first_odd)

    def rs_2(c):
        either(c, rs_second, rs_second_odd)

    def rs_3(c):
        either(c, rs_third, rs_third_odd)

    def rs_4(c):
        either(c, rs_last, rs_last_odd)

    def weight(s, c):
        return jnp.concatenate([wbuf[s, c, 0], wbuf[s, c, 1]], axis=1)

    def compute(c):
        acc = jnp.zeros((B, 2 * B), F32)
        for s in range(0, KEEP, 2):
            lhs = jnp.concatenate([xbuf[rows[s, c]], xbuf[rows[s + 1, c]]], axis=1)
            rhs = jnp.concatenate([weight(s, c), weight(s + 1, c)], axis=0)
            acc = acc + jnp.dot(lhs, rhs, preferred_element_type=F32)
        gate, up = acc[:, :B], acc[:, B:]
        sig = jax.nn.sigmoid(gate)
        silu = gate * sig
        lanes = pl.ds(pl.multiple_of(c * B, B), B)
        hid_ref[:, lanes] = (silu * up).astype(BF16)
        grad = gh_ref[:, lanes].astype(F32)
        d_gate = (grad * up * sig * (1.0 + gate * (1.0 - sig))).astype(BF16)
        d_up = (grad * silu).astype(BF16)
        dt[c, :B] = d_gate.T
        dt[c, B:] = d_up.T
        delta = jnp.concatenate([d_gate, d_up], axis=1)
        for core, target in ((ko, part_out), (k, part)):
            for i in range(0, 8, 2):
                blocks = [xt[rows[slot(*goal[i + half], core), c]] for half in range(2)]
                lhs = jnp.concatenate(blocks, axis=0)
                out = (jnp.dot(lhs, delta, preferred_element_type=F32) * SCALE).astype(BF16)
                for half in range(2):
                    target[c, i + half, 0] = out[half * B : (half + 1) * B, :B]
                    target[c, i + half, 1] = out[half * B : (half + 1) * B, B:]
            if target is part_out:
                rs_pair(c).start()

    def column(c, _):
        @pl.when(c + 3 < NC)
        def _():
            either(c + 3, ag_fourth, ag_fourth_odd)

        ag_end(c)
        compute(c)

        @pl.when(c >= 1)
        def _():
            rs_1(c - 1)

        @pl.when(c >= 3)
        def _():
            rs_2(c - 3)

        return 0

    lax.fori_loop(0, NC, column, 0)

    def unit(zz):
        def one(c, acc):
            lhs = jnp.concatenate([weight(rank[zz * 4 + b, c], c) for b in range(4)], axis=0)
            return acc + jnp.dot(lhs, dt[c], preferred_element_type=F32)

        return lax.fori_loop(0, NC, one, jnp.zeros((4 * B, B), F32)).reshape(4, B, B)

    def ring_copy(src, dst, sem, there):
        return pltpu.make_async_remote_copy(
            src_ref=src, dst_ref=dst, send_sem=dx_ss.at[0], recv_sem=dx_rs.at[sem],
            device_id=there, device_id_type=MESH,
        )

    def go_up(n, half):
        cut = pl.ds(2 * half, 2)
        return ring_copy(up_s.at[n, cut], up_r.at[n, cut], 2 * n + half, to_zp)

    def go_down(n, half):
        cut = pl.ds(2 * half, 2)
        return ring_copy(dn_s.at[n, cut], dn_r.at[n, cut], 8 + 2 * n + half, to_zm)

    far = unit((z + 4) % 8).astype(BF16)
    up_s[0, :2] = far[:2]
    go_up(0, 0).start()
    dn_s[0, 2:] = far[2:]
    go_down(0, 1).start()

    def pass_on(n, go, out, came, mine, order):
        for half in order:
            cut = slice(2 * half, 2 * half + 2)
            value = mine[cut]
            if n > 1 or half == order[1]:
                go(n - 1, half).wait_recv()
                value = value + came[n - 1, cut].astype(F32)
            out[n, cut] = value.astype(BF16)
            go(n, half).start()

    def step(n):
        pass_on(n, go_up, up_s, up_r, unit((z + 4 - n) % 8), (1, 0))
        pass_on(n, go_down, dn_s, dn_r, unit((z + 4 + n) % 8), (0, 1))

    rs_1(6)
    rs_2(4)
    rs_2(5)
    step(1)
    rs_3(0)
    rs_3(1)
    rs_3(2)
    rs_2(6)
    step(2)
    rs_3(3)
    rs_3(4)
    rs_4(0)
    step(3)
    rs_3(5)
    rs_4(1)
    mine = unit(z)
    for half in range(2):
        go_up(3, half).wait_recv()
        go_down(3, half).wait_recv()
    last_s[...] = (mine + up_r[3].astype(F32) + dn_r[3].astype(F32)).astype(BF16)
    across = ring_copy(last_s.at[pl.ds(ho * 2, 2)], last_r, 16, to_h)
    across.start()
    rs_3(6)
    rs_4(2)
    rs_4(3)
    rs_4(4)
    rs_4(5)
    across.wait_recv()
    for b in range(2):
        value = last_s[h * 2 + b].astype(F32) + last_r[b].astype(F32)
        dx_ref[:, b * B : (b + 1) * B] = value.T.astype(BF16)

    rs_4(6)

    def sent(sem):
        pltpu.make_async_remote_copy(
            src_ref=xbuf.at[pl.ds(0, 30)], dst_ref=xbuf.at[pl.ds(0, 30)],
            send_sem=sem, recv_sem=in_r.at[0],
            device_id=to_h, device_id_type=MESH,
        ).wait_send()

    def column_sent(c, _):
        sent(ag_s.at[c])
        sent(rs_s.at[c])
        return 0

    lax.fori_loop(0, NC, column_sent, 0)
    sent(in_s.at[0])
    sent(dx_ss.at[0])


def per_device(inputs, gate_blocks, up_blocks, block_mask, grad_hidden):
    vmem = pl.BlockSpec(memory_space=pltpu.VMEM)
    dma = pltpu.SemaphoreType.DMA
    unit = (4, B, B)
    return pl.pallas_call(
        kernel,
        out_shape=(
            jax.ShapeDtypeStruct(grad_hidden.shape, BF16),
            jax.ShapeDtypeStruct(inputs.shape, BF16),
            jax.ShapeDtypeStruct(gate_blocks.shape, BF16),
            jax.ShapeDtypeStruct(up_blocks.shape, BF16),
        ),
        in_specs=[vmem, vmem, vmem, pl.BlockSpec(memory_space=pltpu.SMEM), vmem],
        out_specs=(vmem, vmem, vmem, vmem),
        scratch_shapes=[
            pltpu.VMEM((KEEP + 1, NC, 2, B, B), BF16),
            pltpu.VMEM((RB, B, B), BF16),
            pltpu.VMEM((RB, B, B), BF16),
            pltpu.VMEM((NC, 2 * B, B), BF16),
            pltpu.VMEM((NC, 8, 2, B, B), BF16),
            pltpu.VMEM((NC, 8, 2, B, B), BF16),
            pltpu.VMEM((NC, 8, 2, B, B), BF16),
            pltpu.VMEM((7, NC, 2, B, B), BF16),
            pltpu.VMEM((7, NC, 2, B, B), BF16),
            pltpu.VMEM((4,) + unit, BF16),
            pltpu.VMEM((4,) + unit, BF16),
            pltpu.VMEM((4,) + unit, BF16),
            pltpu.VMEM((4,) + unit, BF16),
            pltpu.VMEM(unit, BF16),
            pltpu.VMEM((2, B, B), BF16),
            pltpu.SMEM((RB, NC), jnp.int32),
            pltpu.SMEM((KEEP, NC), jnp.int32),
            pltpu.SMEM((RB,), jnp.int32),
            dma((NC,)),
            dma((9, NC)),
            dma((1,)),
            dma((15,)),
            dma((NC,)),
            dma((9, NC)),
            dma((1,)),
            dma((17,)),
        ],
        compiler_params=pltpu.CompilerParams(
            collective_id=0, has_side_effects=True, vmem_limit_bytes=56 * 2**20
        ),
        cost_estimate=pl.CostEstimate(
            flops=4 * 10**9, bytes_accessed=3 * 2**20, transcendentals=128 * 896
        ),
    )(inputs, gate_blocks, up_blocks, block_mask, grad_hidden)


def solution(mesh):
    return jax.shard_map(
        per_device,
        mesh=mesh,
        in_specs=(
            P("dp", "tensor"),
            P("dp", "tensor", None, None),
            P("dp", "tensor", None, None),
            P(None, "tensor"),
            P("dp", "tensor"),
        ),
        out_specs=(
            P("dp", "tensor"),
            P("dp", "tensor"),
            P("dp", "tensor", None, None),
            P("dp", "tensor", None, None),
        ),
        check_vma=False,
    )
```

```python
import jax
import jax.numpy as jnp
from jax import lax
from jax.experimental import pallas as pl
from jax.experimental.pallas import tpu as pltpu
from jax.sharding import PartitionSpec as P

MESH = pl.DeviceIdType.MESH
F32, BF16 = jnp.float32, jnp.bfloat16
B = 128
NC = 7
KEEP = 16
RB = 32
SCALE = 2048.0**-0.5


def kernel(
    x_ref, g_ref, u_ref, mask_ref, gh_ref,
    hid_ref, dx_ref, gg_ref, gu_ref,
    wbuf, xbuf, xt, dt, part_out, part_in, part, leave, land, up_s, up_r, dn_s, dn_r, last_s, last_r,
    rank, rows, following,
    ag_s, ag_r, in_s, in_r, rs_s, rs_r, dx_ss, dx_rs,
):
    dp, tn = lax.axis_index("dp"), lax.axis_index("tensor")
    y, x, k = dp // 4, (dp // 2) % 2, dp % 2
    z, h = tn // 2, tn % 2
    yp, ym, y2 = (y + 1) % 4, (y + 3) % 4, (y + 2) % 4
    zp, zm = (z + 1) % 8, (z + 7) % 8
    xo, ko, ho = 1 - x, 1 - k, 1 - h

    def slot(yy, xx, kk):
        return yy * 4 + xx * 2 + kk

    to_sib = (slot(y, x, ko), tn)
    to_x = (slot(y, xo, k), tn)
    to_yp = (slot(yp, x, k), tn)
    to_ym = (slot(ym, x, k), tn)
    to_zp = (dp, zp * 2 + h)
    to_zm = (dp, zm * 2 + h)
    to_h = (dp, z * 2 + ho)
    neighbours = (to_sib, to_x, to_yp, to_ym, to_zp, to_zm, to_h)

    barrier = pltpu.get_barrier_semaphore()
    for there in neighbours:
        pl.semaphore_signal(barrier, inc=1, device_id=there, device_id_type=MESH)

    for c in range(NC):
        wbuf[dp, c, 0] = g_ref[0, c]
        wbuf[dp, c, 1] = u_ref[0, c]
        wbuf[KEEP, c] = jnp.zeros((2, B, B), BF16)
    for b in range(2):
        xbuf[tn * 2 + b] = x_ref[:, b * B : (b + 1) * B]
    pl.semaphore_wait(barrier, len(neighbours))

    ring = ((y, x), (y, xo), (ym, x), (yp, x), (ym, xo), (yp, xo), (y2, x), (y2, xo))
    OWN, N, PP, MM, NP, NM, P2, M2 = range(8)

    def ag(kind, which, c, there, core):
        s = slot(*ring[which], core)
        return pltpu.make_async_remote_copy(
            src_ref=wbuf.at[s, c], dst_ref=wbuf.at[s, c],
            send_sem=ag_s.at[c], recv_sem=ag_r.at[min(kind, 8), c],
            device_id=there, device_id_type=MESH,
        )

    def ag_send(kind, which, c, there):
        ag(kind, which, c, there, k).start()

    def ag_got(kind, c):
        ag(kind, kind, c, to_x, k).wait_recv()

    def ag_share(which, c):
        ag(8 + which, which, c, to_sib, k).start()

    def ag_own(c):
        ag_send(N, OWN, c, to_x)
        ag_send(PP, OWN, c, to_yp)
        ag_send(MM, OWN, c, to_ym)
        ag_share(OWN, c)

    def ag_second(c):
        ag_got(N, c)
        ag_send(NP, N, c, to_yp)
        ag_send(NM, N, c, to_ym)
        ag_share(N, c)

    def ag_third(c):
        ag_got(PP, c)
        ag_send(P2, PP, c, to_yp)
        ag_share(PP, c)
        ag_got(MM, c)
        ag_share(MM, c)
        ag_got(NM, c)
        ag_send(M2, NM, c, to_ym)
        ag_share(NM, c)
        ag_got(NP, c)
        ag_share(NP, c)

    def ag_fourth(c):
        ag_got(P2, c)
        ag_share(P2, c)
        ag_got(M2, c)
        ag_share(M2, c)

    HALF = 0

    def ag_half(kind, which, c, half, there):
        s = slot(*ring[which], k)
        return pltpu.make_async_remote_copy(
            src_ref=wbuf.at[s, c, half], dst_ref=wbuf.at[s, c, half],
            send_sem=ag_s.at[c], recv_sem=ag_r.at[kind, c],
            device_id=there, device_id_type=MESH,
        )

    def ag_second_odd(c):
        ag_got(PP, c)
        ag_half(P2, PP, c, 0, to_yp).start()
        ag_send(NP, PP, c, to_x)
        ag_share(PP, c)
        ag_got(MM, c)
        ag_half(HALF, MM, c, 1, to_ym).start()
        ag_send(NM, MM, c, to_x)
        ag_share(MM, c)
        ag_got(N, c)
        ag_share(N, c)

    def ag_third_odd(c):
        ag_half(P2, P2, c, 0, to_yp).wait_recv()
        ag_half(HALF, P2, c, 1, to_ym).wait_recv()
        ag_send(M2, P2, c, to_x)
        ag_share(P2, c)
        ag_got(NP, c)
        ag_share(NP, c)
        ag_got(NM, c)
        ag_share(NM, c)

    def ag_fourth_odd(c):
        ag_got(M2, c)
        ag_share(M2, c)

    def either(c, even, odd):
        if isinstance(c, int):
            (odd if c % 2 else even)(c)
        else:
            pl.when(c % 2 == 0)(lambda: even(c))
            pl.when(c % 2 == 1)(lambda: odd(c))

    def ag_end(c):
        pltpu.make_async_remote_copy(
            src_ref=part_in.at[c], dst_ref=part_in.at[c],
            send_sem=ag_s.at[c], recv_sem=ag_r.at[8, c],
            device_id=to_sib, device_id_type=MESH,
        ).wait_recv()

    def inp(sem, zz, hh, there):
        at = pl.ds(((zz + 8) % 8) * 4 + hh * 2, 2)
        return pltpu.make_async_remote_copy(
            src_ref=xbuf.at[at], dst_ref=xbuf.at[at],
            send_sem=in_s.at[0], recv_sem=in_r.at[sem],
            device_id=there, device_id_type=MESH,
        )

    own_up, oth_dn, own_dn, oth_up = 0, 4, 8, 11

    inp(0, z, h, to_h).start()
    inp(own_up + 1, z, h, to_zp).start()
    inp(own_dn + 1, z, h, to_zm).start()
    for c in range(NC):
        ag_own(c)

    inp(0, z, ho, to_h).wait_recv()
    inp(oth_up + 1, z, ho, to_zp).start()
    inp(oth_dn + 1, z, ho, to_zm).start()

    def column_tables(c, _):
        def count(r, seen):
            here = mask_ref[r, c]
            rank[r, c] = jnp.where(here == 1, jnp.minimum(seen, KEEP - 1), KEEP)
            return seen + here

        lax.fori_loop(0, RB, count, jnp.int32(0))

        def back(q, after):
            r = RB - 1 - q
            after = jnp.where(mask_ref[r, c] == 1, r, after)
            following[r] = after
            return after

        lax.fori_loop(0, RB, back, jnp.int32(RB - 1))

        def pick(kk, r):
            r = following[jnp.minimum(r, RB - 1)]
            rows[kk, c] = r
            return r + 1

        lax.fori_loop(0, KEEP, pick, jnp.int32(0))
        return 0

    lax.fori_loop(0, NC, column_tables, 0)

    for j in (1, 2, 3, 4):
        inp(own_up + j, z - j, h, to_zp).wait_recv()
        if j < 4:
            inp(own_up + j + 1, z - j, h, to_zp).start()
        if j < 4:
            inp(own_dn + j, z + j, h, to_zm).wait_recv()
            if j < 3:
                inp(own_dn + j + 1, z + j, h, to_zm).start()
            inp(oth_up + j, z - j, ho, to_zp).wait_recv()
            if j < 3:
                inp(oth_up + j + 1, z - j, ho, to_zp).start()
        inp(oth_dn + j, z + j, ho, to_zm).wait_recv()
        if j < 4:
            inp(oth_dn + j + 1, z + j, ho, to_zm).start()
        for c in ((), (0, 1, 2), (3, 4, 5, 6), (), ())[j]:
            either(c, ag_second, ag_second_odd)
        for c in ((), (), (0,), (1, 2, 3), (4, 5))[j]:
            either(c, ag_third, ag_third_odd)
        for c in ((), (), (), (0,), (1,))[j]:
            either(c, ag_fourth, ag_fourth_odd)

    def turn(r, _):
        xt[r] = xbuf[r].T
        return 0

    lax.fori_loop(0, RB, turn, 0)
    ag_third(6)
    ag_fourth(2)

    A_UP, A_DN, C_UP, C_DN, E_UP, F_DN, G_X = range(7)

    goal = ((y2, x), (y2, xo), (yp, xo), (ym, x), (yp, x), (ym, xo), (y, xo), (y, x))
    MINE = 7

    def rs(kind, c, there):
        return pltpu.make_async_remote_copy(
            src_ref=leave.at[kind, c], dst_ref=land.at[kind, c],
            send_sem=rs_s.at[c], recv_sem=rs_r.at[kind, c],
            device_id=there, device_id_type=MESH,
        )

    def rs_pair(c):
        return pltpu.make_async_remote_copy(
            src_ref=part_out.at[c], dst_ref=part_in.at[c],
            send_sem=rs_s.at[c], recv_sem=rs_r.at[7, c],
            device_id=to_sib, device_id_type=MESH,
        )

    def rs_got(kind, c):
        rs(kind, c, to_x).wait_recv()

    def total(c, goes, kinds):
        value = part[c, goes].astype(F32) + part_in[c, goes].astype(F32)
        for kind in kinds:
            value = value + land[kind, c].astype(F32)
        return value

    def rs_send(kind, c, there, kinds=()):
        leave[kind, c] = total(c, kind, kinds).astype(BF16)
        rs(kind, c, there).start()

    def rs_first(c):
        rs_pair(c).wait_recv()
        rs_send(A_UP, c, to_yp)
        rs_send(A_DN, c, to_ym)
        rs_send(C_UP, c, to_yp)
        rs_send(C_DN, c, to_ym)

    def rs_second(c):
        rs_got(A_UP, c)
        rs_send(E_UP, c, to_yp, (A_UP,))
        rs_got(A_DN, c)
        rs_send(F_DN, c, to_ym, (A_DN,))

    def rs_third(c):
        rs_got(C_UP, c)
        rs_got(F_DN, c)
        rs_send(G_X, c, to_x, (C_UP, F_DN))

    def rs_last(c):
        for kind in (C_DN, E_UP, G_X):
            rs_got(kind, c)
        value = total(c, MINE, (C_DN, E_UP, G_X)).astype(BF16)
        gg_ref[0, c] = value[0]
        gu_ref[0, c] = value[1]

    X_Y2, X_YP, X_YM, X_Y, TO_UP, TO_DN, HALF_DN = 1, 2, 5, 6, 4, 3, 8

    def rs_half(c, half):
        there, sem = ((to_yp, 0), (to_ym, HALF_DN))[half]
        return pltpu.make_async_remote_copy(
            src_ref=leave.at[0, c, half], dst_ref=land.at[0, c, half],
            send_sem=rs_s.at[c], recv_sem=rs_r.at[sem, c],
            device_id=there, device_id_type=MESH,
        )

    def rs_first_odd(c):
        rs_pair(c).wait_recv()
        for kind in (X_Y2, X_YP, X_YM, X_Y):
            rs_send(kind, c, to_x)

    def rs_second_odd(c):
        rs_got(X_Y2, c)
        leave[0, c] = total(c, 0, (X_Y2,)).astype(BF16)
        rs_half(c, 0).start()
        rs_half(c, 1).start()

    def rs_third_odd(c):
        for kind, came, half, there in ((TO_UP, X_YP, 0, to_yp), (TO_DN, X_YM, 1, to_ym)):
            rs_got(came, c)
            value = total(c, kind, (came,))
            rs_half(c, half).wait_recv()
            leave[kind, c, half] = (value[half] + land[0, c, half].astype(F32)).astype(BF16)
            leave[kind, c, 1 - half] = value[1 - half].astype(BF16)
            rs(kind, c, there).start()

    def rs_last_odd(c):
        for kind in (X_Y, TO_UP, TO_DN):
            rs_got(kind, c)
        value = total(c, MINE, (X_Y, TO_UP, TO_DN)).astype(BF16)
        gg_ref[0, c] = value[0]
        gu_ref[0, c] = value[1]

    def rs_1(c):
        either(c, rs_first, rs_first_odd)

    def rs_2(c):
        either(c, rs_second, rs_second_odd)

    def rs_3(c):
        either(c, rs_third, rs_third_odd)

    def rs_4(c):
        either(c, rs_last, rs_last_odd)

    def weight(s, c):
        return jnp.concatenate([wbuf[s, c, 0], wbuf[s, c, 1]], axis=1)

    def compute(c):
        acc = jnp.zeros((B, 2 * B), F32)
        for s in range(0, KEEP, 2):
            lhs = jnp.concatenate([xbuf[rows[s, c]], xbuf[rows[s + 1, c]]], axis=1)
            rhs = jnp.concatenate([weight(s, c), weight(s + 1, c)], axis=0)
            acc = acc + jnp.dot(lhs, rhs, preferred_element_type=F32)
        gate, up = acc[:, :B], acc[:, B:]
        sig = jax.nn.sigmoid(gate)
        silu = gate * sig
        lanes = pl.ds(pl.multiple_of(c * B, B), B)
        hid_ref[:, lanes] = (silu * up).astype(BF16)
        grad = gh_ref[:, lanes].astype(F32)
        d_gate = (grad * up * sig * (1.0 + gate * (1.0 - sig))).astype(BF16)
        d_up = (grad * silu).astype(BF16)
        dt[c, :B] = d_gate.T
        dt[c, B:] = d_up.T
        delta = jnp.concatenate([d_gate, d_up], axis=1)
        for core, target in ((ko, part_out), (k, part)):
            for i in range(0, 8, 2):
                blocks = [xt[rows[slot(*goal[i + half], core), c]] for half in range(2)]
                lhs = jnp.concatenate(blocks, axis=0)
                out = (jnp.dot(lhs, delta, preferred_element_type=F32) * SCALE).astype(BF16)
                for half in range(2):
                    target[c, i + half, 0] = out[half * B : (half + 1) * B, :B]
                    target[c, i + half, 1] = out[half * B : (half + 1) * B, B:]
            if target is part_out:
                rs_pair(c).start()

    def column(c, _):
        @pl.when(c + 3 < NC)
        def _():
            either(c + 3, ag_fourth, ag_fourth_odd)

        ag_end(c)
        compute(c)

        @pl.when(c >= 1)
        def _():
            rs_1(c - 1)

        @pl.when(c >= 3)
        def _():
            rs_2(c - 3)

        return 0

    lax.fori_loop(0, NC, column, 0)

    def unit(zz):
        def one(c, acc):
            lhs = jnp.concatenate([weight(rank[zz * 4 + b, c], c) for b in range(4)], axis=0)
            return acc + jnp.dot(lhs, dt[c], preferred_element_type=F32)

        return lax.fori_loop(0, NC, one, jnp.zeros((4 * B, B), F32)).reshape(4, B, B)

    def ring_copy(src, dst, sem, there):
        return pltpu.make_async_remote_copy(
            src_ref=src, dst_ref=dst, send_sem=dx_ss.at[0], recv_sem=dx_rs.at[sem],
            device_id=there, device_id_type=MESH,
        )

    def go_up(n, half):
        cut = pl.ds(2 * half, 2)
        return ring_copy(up_s.at[n, cut], up_r.at[n, cut], 2 * n + half, to_zp)

    def go_down(n, half):
        cut = pl.ds(2 * half, 2)
        return ring_copy(dn_s.at[n, cut], dn_r.at[n, cut], 8 + 2 * n + half, to_zm)

    far = unit((z + 4) % 8).astype(BF16)
    up_s[0, :2] = far[:2]
    go_up(0, 0).start()
    dn_s[0, 2:] = far[2:]
    go_down(0, 1).start()

    def pass_on(n, go, out, came, mine, order):
        for half in order:
            cut = slice(2 * half, 2 * half + 2)
            value = mine[cut]
            if n > 1 or half == order[1]:
                go(n - 1, half).wait_recv()
                value = value + came[n - 1, cut].astype(F32)
            out[n, cut] = value.astype(BF16)
            go(n, half).start()

    def step(n):
        pass_on(n, go_up, up_s, up_r, unit((z + 4 - n) % 8), (1, 0))
        pass_on(n, go_down, dn_s, dn_r, unit((z + 4 + n) % 8), (0, 1))

    rs_1(6)
    rs_2(4)
    step(1)
    rs_2(5)
    rs_3(0)
    rs_3(1)
    rs_2(6)
    step(2)
    rs_3(2)
    rs_3(3)
    step(3)
    rs_3(4)
    rs_3(5)
    mine = unit(z)
    for half in range(2):
        go_up(3, half).wait_recv()
        go_down(3, half).wait_recv()
    last_s[...] = (mine + up_r[3].astype(F32) + dn_r[3].astype(F32)).astype(BF16)
    across = ring_copy(last_s.at[pl.ds(ho * 2, 2)], last_r, 16, to_h)
    across.start()
    rs_3(6)
    rs_4(0)
    rs_4(1)
    rs_4(2)
    rs_4(3)
    rs_4(4)
    rs_4(5)
    across.wait_recv()
    for b in range(2):
        value = last_s[h * 2 + b].astype(F32) + last_r[b].astype(F32)
        dx_ref[:, b * B : (b + 1) * B] = value.T.astype(BF16)

    rs_4(6)

    def sent(sem):
        pltpu.make_async_remote_copy(
            src_ref=xbuf.at[pl.ds(0, 30)], dst_ref=xbuf.at[pl.ds(0, 30)],
            send_sem=sem, recv_sem=in_r.at[0],
            device_id=to_h, device_id_type=MESH,
        ).wait_send()

    def column_sent(c, _):
        sent(ag_s.at[c])
        sent(rs_s.at[c])
        return 0

    lax.fori_loop(0, NC, column_sent, 0)
    sent(in_s.at[0])
    sent(dx_ss.at[0])


def per_device(inputs, gate_blocks, up_blocks, block_mask, grad_hidden):
    vmem = pl.BlockSpec(memory_space=pltpu.VMEM)
    dma = pltpu.SemaphoreType.DMA
    unit = (4, B, B)
    return pl.pallas_call(
        kernel,
        out_shape=(
            jax.ShapeDtypeStruct(grad_hidden.shape, BF16),
            jax.ShapeDtypeStruct(inputs.shape, BF16),
            jax.ShapeDtypeStruct(gate_blocks.shape, BF16),
            jax.ShapeDtypeStruct(up_blocks.shape, BF16),
        ),
        in_specs=[vmem, vmem, vmem, pl.BlockSpec(memory_space=pltpu.SMEM), vmem],
        out_specs=(vmem, vmem, vmem, vmem),
        scratch_shapes=[
            pltpu.VMEM((KEEP + 1, NC, 2, B, B), BF16),
            pltpu.VMEM((RB, B, B), BF16),
            pltpu.VMEM((RB, B, B), BF16),
            pltpu.VMEM((NC, 2 * B, B), BF16),
            pltpu.VMEM((NC, 8, 2, B, B), BF16),
            pltpu.VMEM((NC, 8, 2, B, B), BF16),
            pltpu.VMEM((NC, 8, 2, B, B), BF16),
            pltpu.VMEM((7, NC, 2, B, B), BF16),
            pltpu.VMEM((7, NC, 2, B, B), BF16),
            pltpu.VMEM((4,) + unit, BF16),
            pltpu.VMEM((4,) + unit, BF16),
            pltpu.VMEM((4,) + unit, BF16),
            pltpu.VMEM((4,) + unit, BF16),
            pltpu.VMEM(unit, BF16),
            pltpu.VMEM((2, B, B), BF16),
            pltpu.SMEM((RB, NC), jnp.int32),
            pltpu.SMEM((KEEP, NC), jnp.int32),
            pltpu.SMEM((RB,), jnp.int32),
            dma((NC,)),
            dma((9, NC)),
            dma((1,)),
            dma((15,)),
            dma((NC,)),
            dma((9, NC)),
            dma((1,)),
            dma((17,)),
        ],
        compiler_params=pltpu.CompilerParams(
            collective_id=0, has_side_effects=True, vmem_limit_bytes=56 * 2**20
        ),
        cost_estimate=pl.CostEstimate(
            flops=4 * 10**9, bytes_accessed=3 * 2**20, transcendentals=128 * 896
        ),
    )(inputs, gate_blocks, up_blocks, block_mask, grad_hidden)


def solution(mesh):
    return jax.shard_map(
        per_device,
        mesh=mesh,
        in_specs=(
            P("dp", "tensor"),
            P("dp", "tensor", None, None),
            P("dp", "tensor", None, None),
            P(None, "tensor"),
            P("dp", "tensor"),
        ),
        out_specs=(
            P("dp", "tensor"),
            P("dp", "tensor"),
            P("dp", "tensor", None, None),
            P("dp", "tensor", None, None),
        ),
        check_vma=False,
    )
```
